32 devices in a mesh: rows: 8 (over y, x, core), cols: 4 (over z).
Axes of the slice: x: 2, y: 2, z: 4, core: 2. Of those that a mesh axis runs over, the one named last changes fastest.
Arguments:
- owner_map: int32 [2, 128], replicated, may hold values from 0 to 127, as said below
- colidx: int32 [2, 128, 24], P(None, 'rows', 'cols'), may hold values from 0 to 191, as said below
- live: int32 [2, 128], P(None, 'rows'), may hold values from 1 to 24
- blocks: bfloat16 [2, 128, 24, 128, 128], P(None, 'rows', 'cols'), may hold values from -0.15625 to 0.15625
- diag_inverse: float32 [2, 128, 128, 128], P(None, 'rows')
- right_side: float32 [2, 128, 64, 128], P(None, 'rows'), may hold values from -6 to 6
- prior: bfloat16 [64, 64, 128], P('rows'), may hold values from -6 to 6
Outputs:
- solved: float32 [2, 128, 64, 128], P(None, 'rows')
The draws below stay inside these ranges and needn't reach their ends.
Inputs may be any that keep to these rules, and one draw needn't show every extreme that they name: Each row of owner_map is a permutation of the block rows of a front. `colidx`: front 0 refers only to earlier block rows; in front 1, even slots refer to rows of front 0 and odd slots to earlier block rows. Take the even slots of front 1 that lie in block rows s with s // 16 equal to one value and in slots j with j // 6 equal to one value. Among them, at most 6 refer to front-0 rows r whose slot t (owner_map[0, t] = r) has t // 16 equal to any single value; some such group reaches 6.
All inputs are finite; a program needn't handle non-finite values.
Results may differ from the reference program's by a relative error of at most 0.0017.
Values may be sent and summed in bfloat16 or wider, within the bound.
No kernel may reach another device: no remote copies, remote signals or barrier semaphores. Data moves between devices by JAX's collectives and lax.ppermute only.
A program may use at most 64 MiB of HBM per device.

```python
import jax
import jax.numpy as jnp
from jax import lax

B = 128
P_SIZE = 64
NB = 24
ROWS_DEV = 16
ROWS_F = 128
NPRI = 64
NBC = 6
CAP = 6


def draw_owner_map(key, part):
    first = jax.random.permutation(jax.random.fold_in(key, 11), ROWS_F)
    second = jax.random.permutation(jax.random.fold_in(key, 12), ROWS_F)
    row_groups = ROWS_F // ROWS_DEV
    col_groups = NB // NBC
    per_block = ROWS_DEV * NBC
    shift = jax.random.randint(jax.random.fold_in(key, 25), (row_groups, col_groups, 1), 0, row_groups)
    within = jax.random.randint(jax.random.fold_in(key, 26), (row_groups, col_groups, per_block), 0, ROWS_DEV)
    target = shift[0, 0, 0] * ROWS_DEV + within[0, 0, 0]
    held = first[target]
    where_top = jnp.argmax(first == ROWS_F - 1)
    first = first.at[where_top].set(held).at[target].set(ROWS_F - 1)
    return jnp.stack([first, second]).astype(jnp.int32)


def draw_colidx(key, part):
    owner_map = draw_owner_map(key, part)
    early_a = jax.random.randint(jax.random.fold_in(key, 21), (ROWS_F, NB), 0, NPRI)
    early_b = jax.random.randint(jax.random.fold_in(key, 22), (ROWS_F, NB), 0, NPRI)
    row_groups = ROWS_F // ROWS_DEV
    col_groups = NB // NBC
    per_block = ROWS_DEV * NBC
    spread = row_groups * CAP
    slot_ids = jnp.arange(col_groups)[:, None, None] * NBC + jnp.arange(NBC)[None, None, :]
    even = jnp.broadcast_to(slot_ids % 2 == 0, (col_groups, ROWS_DEV, NBC)).reshape(col_groups, per_block)
    rank = jnp.clip(jnp.cumsum(even.astype(jnp.int32), axis=-1) - 1, 0, spread - 1)
    scores = jax.random.randint(jax.random.fold_in(key, 24), (row_groups, col_groups, spread), 0, 65536)
    scores = scores * spread + jnp.arange(spread)
    scores = jnp.where(jnp.arange(spread) < CAP, jnp.arange(spread) - CAP, scores)
    order = jnp.argsort(scores, axis=-1)
    rank_all = jnp.broadcast_to(rank[None], (row_groups, col_groups, per_block))
    holders = jnp.take_along_axis(order, rank_all, axis=-1) // CAP
    shift = jax.random.randint(jax.random.fold_in(key, 25), (row_groups, col_groups, 1), 0, row_groups)
    holders = (holders + shift) % row_groups
    within = jax.random.randint(jax.random.fold_in(key, 26), (row_groups, col_groups, per_block), 0, ROWS_DEV)
    recent = NPRI + owner_map[0][holders * ROWS_DEV + within]
    recent = recent.reshape(row_groups, col_groups, ROWS_DEV, NBC).transpose(0, 2, 1, 3).reshape(ROWS_F, NB)
    even_full = jnp.broadcast_to((jnp.arange(NB) % 2 == 0)[None, :], (ROWS_F, NB))
    second = jnp.where(even_full, recent, early_b)
    early_a = early_a.at[0, 0].set(0)
    return jnp.stack([early_a, second]).astype(jnp.int32)


def draw_live(key, part):
    counts = jax.random.randint(jax.random.fold_in(key, 31), (2, ROWS_F), 1, NB + 1)
    pick = jax.random.randint(jax.random.fold_in(key, 32), (2, ROWS_F), 0, 4)
    counts = jnp.where(pick == 0, NB, counts)
    counts = counts.at[:, 0].set(NB).at[:, 1].set(1)
    return counts.astype(jnp.int32)


def draw_diag_inverse(key, part):
    eye = jnp.eye(B, dtype=jnp.float32)
    diag = jax.random.uniform(jax.random.fold_in(key, 41), (2, ROWS_F, 1, B), jnp.float32, 0.8, 1.2)
    rest = 0.05 * jax.random.normal(jax.random.fold_in(key, 42), (2, ROWS_F, B, B), jnp.float32)
    return (eye * diag + rest).astype(jnp.float32)


def block_levels(stream_key, extent, shards, least, high):
    def one(position, blocks):
        draws = jax.random.uniform(jax.random.fold_in(jax.random.fold_in(stream_key, 6), position), (blocks,), jnp.float32, least / len(shards), high / len(shards))
        return jnp.repeat(jnp.exp(draws), extent[position] // blocks).reshape((-1,) + (1,) * (len(extent) - position - 1))

    loudness = one(*shards[0])
    for cut in shards[1:]:
        loudness = loudness * one(*cut)
    return loudness


def normal_values(own_key, extent, scale, limit, pieces=(), kind=jnp.bfloat16):
    array = jax.random.normal(own_key, extent, jnp.float32) * scale
    if len(pieces) > 0:
        array = block_levels(own_key, extent, pieces, -0.22, 0.18) * array
    return jnp.clip(array, min=-limit, max=limit).astype(kind)


def setup_inputs(seed: int = 0) -> dict:
    key_list = jax.random.split(jax.random.key(seed), 8)
    return {
        "owner_map": draw_owner_map(jax.random.fold_in(key_list[7], 71), 0),
        "colidx": draw_colidx(jax.random.fold_in(key_list[7], 71), 0),
        "live": draw_live(jax.random.fold_in(key_list[7], 71), 0),
        "blocks": normal_values(key_list[3], (2, ROWS_F, NB, B, B), (B * NB // 2) ** -0.5, 0.15625, ((1, 8), (2, 4))),
        "diag_inverse": draw_diag_inverse(jax.random.fold_in(key_list[7], 71), 0),
        "right_side": normal_values(key_list[5], (2, ROWS_F, P_SIZE, B), 1.0, 6.0, ((1, 8),), jnp.float32),
        "prior": normal_values(key_list[6], (NPRI, P_SIZE, B), 1.0, 6.0, ((0, 8),)),
    }


def solve_front(front, known, colidx, live, blocks, diag_inverse, right_side):
    slots = jnp.arange(NB)
    mask = slots[None, :] < live[front][:, None]

    def one_row(items):
        blk, idx, keep, rhs, inverse = items
        xs = jnp.where(keep[:, None, None], known[idx], jnp.zeros((), known.dtype)).astype(jnp.float32)
        total = jnp.einsum("jcb,jpb->pc", blk.astype(jnp.float32), xs)
        resid = rhs - total
        return jnp.einsum("pb,cb->pc", resid, inverse, precision=lax.Precision.HIGHEST)

    return lax.map(one_row, (blocks[front], colidx[front], mask, right_side[front], diag_inverse[front]))


def reference(owner_map, colidx, live, blocks, diag_inverse, right_side, prior):
    first = solve_front(0, prior, colidx, live, blocks, diag_inverse, right_side)
    placed = jnp.zeros_like(first).at[owner_map[0]].set(first).astype(jnp.bfloat16)
    known = jnp.concatenate([prior, placed], axis=0)
    second = solve_front(1, known, colidx, live, blocks, diag_inverse, right_side)
    return jnp.stack([first, second])
```

```python
import functools

import jax
import jax.numpy as jnp
from jax import lax
from jax.experimental import pallas as pl
from jax.experimental.pallas import tpu as pltpu
from jax.sharding import PartitionSpec as P

F32, BF16, I32, I16 = jnp.float32, jnp.bfloat16, jnp.int32, jnp.int16
VMEM = pl.BlockSpec(memory_space=pltpu.VMEM)
SMEM = pl.BlockSpec(memory_space=pltpu.SMEM)
ANY = pl.BlockSpec(memory_space=pl.ANY)
STEPS = 128.0
TAIL = 16


def encode_blocks(values, msg_ref, probes):
    rows = lax.broadcasted_iota(I32, (TAIL, msg_ref.shape[1]), 0)
    tail = jnp.zeros((TAIL, msg_ref.shape[1]), F32)
    for k, value in enumerate(values):
        peak = jnp.maximum(jnp.max(jnp.abs(value), keepdims=True), 2.0**-100)
        level = jnp.ceil(jnp.log2(peak) * STEPS)
        scaled = jnp.round(value * jnp.exp2(15.0 - level * (1.0 / STEPS)))
        scaled = jnp.clip(scaled, -32767.0, 32767.0)
        msg_ref[k * probes : (k + 1) * probes] = scaled.astype(I32).astype(I16)
        tail = jnp.where(rows == k, level, tail)
    msg_ref[len(values) * probes :] = tail.astype(I32).astype(I16)


def decode_blocks(msg_ref, count, probes):
    tail = msg_ref[count * probes :].astype(I32).astype(F32)
    factor = jnp.exp2(tail * (1.0 / STEPS) - 15.0)
    return [
        msg_ref[k * probes : (k + 1) * probes].astype(I32).astype(F32) * factor[k : k + 1]
        for k in range(count)
    ]


def partial_kernel(front, cols, n_in, idx_ref, blocks_ref, *refs):
    ins, own_ref, msgs = refs[:n_in], refs[n_in], refs[n_in + 1 : n_in + cols]
    blk, known, sems = refs[n_in + cols :]
    _, rows_dev, slots, order, _ = blocks_ref.shape
    part = rows_dev // cols
    probes = own_ref.shape[1]
    here = idx_ref[rows_dev * slots]
    copies = []
    for s in range(cols):
        first = lax.rem(here + s, cols) * part
        copy = pltpu.make_async_copy(
            blocks_ref.at[front, pl.ds(first, part)], blk.at[pl.ds(s * part, part)], sems.at[s]
        )
        copy.start()
        copies.append(copy)
    at = 0
    for ref in ins:
        known[at : at + ref.shape[0]] = ref[...]
        at += ref.shape[0]
    known[at] = jnp.zeros(known.shape[1:], known.dtype)
    for s in list(range(1, cols)) + [0]:
        copies[s].wait()
        first = lax.rem(here + s, cols) * part
        sums = []
        for k in range(part):
            xs = [known[idx_ref[(first + k) * slots + j]] for j in range(slots)]
            ws = [blk[s * part + k, j] for j in range(slots)]
            sums.append(
                lax.dot_general(
                    jnp.concatenate(xs, axis=1),
                    jnp.concatenate(ws, axis=1),
                    (((1,), (1,)), ((), ())),
                    preferred_element_type=F32,
                )
            )
        if s == 0:
            for k in range(part):
                own_ref[k] = sums[k]
        else:
            encode_blocks(sums, msgs[s - 1], probes)


def partial_products(front, cols, idx, blocks, ins):
    _, rows_dev, slots, order, _ = blocks.shape
    part = rows_dev // cols
    probes = ins[0].shape[1]
    known_rows = sum(a.shape[0] for a in ins) + 1
    msg = jax.ShapeDtypeStruct((part * probes + TAIL, order), I16)
    out = pl.pallas_call(
        functools.partial(partial_kernel, front, cols, len(ins)),
        out_shape=[jax.ShapeDtypeStruct((part, probes, order), F32)] + [msg] * (cols - 1),
        in_specs=[SMEM, ANY] + [VMEM] * len(ins),
        out_specs=[VMEM] * cols,
        scratch_shapes=[
            pltpu.VMEM((rows_dev, slots, order, order), BF16),
            pltpu.VMEM((known_rows, probes, order), BF16),
            pltpu.SemaphoreType.DMA((cols,)),
        ],
        compiler_params=pltpu.CompilerParams(vmem_limit_bytes=32 * 2**20),
        name=f"partial_{front}",
    )(idx, blocks, *ins)
    return out[0], out[1:]


def solve_kernel(cols, own_ref, *refs):
    msgs, rhs_ref, inv_ref, out_ref = refs[: cols - 1], refs[cols - 1], refs[cols], refs[cols + 1]
    part, probes, _ = own_ref.shape
    total = [own_ref[k] for k in range(part)]
    for msg in msgs:
        total = [a + b for a, b in zip(total, decode_blocks(msg, part, probes))]
    solved = [
        lax.dot_general(
            rhs_ref[k] - total[k],
            inv_ref[k],
            (((1,), (1,)), ((), ())),
            precision=lax.Precision.HIGHEST,
            preferred_element_type=F32,
        )
        for k in range(part)
    ]
    encode_blocks(solved, out_ref, probes)


def solve_part(cols, own, msgs, rhs, inverse):
    part, probes, order = own.shape
    return pl.pallas_call(
        functools.partial(solve_kernel, cols),
        out_shape=jax.ShapeDtypeStruct((part * probes + TAIL, order), I16),
        in_specs=[VMEM] * (cols + 2),
        out_specs=VMEM,
        name="solve",
    )(own, *msgs, rhs, inverse)


def pack_kernel(cols, groups, cap, sel_ref, *refs):
    msgs, out_ref, sends, rows = refs[:cols], refs[cols], refs[cols + 1 : -1], refs[-1]
    part = rows.shape[0] // cols
    probes = rows.shape[1]
    here = sel_ref[groups * cap]
    for s in range(cols):
        first = lax.rem(here + cols - s, cols) * part
        for k, value in enumerate(decode_blocks(msgs[s], part, probes)):
            out_ref[0, first + k] = value
            rows[first + k] = value.astype(BF16)
    for m in range(groups):
        for q in range(cap):
            sends[m][q] = rows[sel_ref[m * cap + q]]


def pack(cols, groups, cap, sel, msgs, shape):
    _, rows_dev, probes, order = shape
    out = pl.pallas_call(
        functools.partial(pack_kernel, cols, groups, cap),
        out_shape=[jax.ShapeDtypeStruct(shape, F32)]
        + [jax.ShapeDtypeStruct((cap, probes, order), BF16)] * groups,
        in_specs=[SMEM] + [VMEM] * cols,
        out_specs=[VMEM] * (groups + 1),
        scratch_shapes=[pltpu.VMEM((rows_dev, probes, order), BF16)],
        name="pack",
    )(sel, *msgs)
    return out[0], out[1:]


def last_kernel(cols, here_ref, first_ref, *refs):
    msgs, out_ref = refs[:cols], refs[cols]
    part = out_ref.shape[1] // cols
    probes = out_ref.shape[2]
    out_ref[0] = first_ref[0]
    for s in range(cols):
        first = lax.rem(here_ref[0] + cols - s, cols) * part
        for k, value in enumerate(decode_blocks(msgs[s], part, probes)):
            out_ref[1, first + k] = value


def last(cols, here, first, msgs, shape):
    return pl.pallas_call(
        functools.partial(last_kernel, cols),
        out_shape=jax.ShapeDtypeStruct(shape, F32),
        in_specs=[SMEM, VMEM] + [VMEM] * cols,
        out_specs=VMEM,
        name="last",
    )(here, first, *msgs)


def shards(groups, cols, owner_map, colidx, live, blocks, diag_inverse, right_side, prior):
    _, rows_dev, slots, order, _ = blocks.shape
    probes = right_side.shape[2]
    prior_dev = prior.shape[0]
    prior_count = groups * prior_dev
    half = groups // 2
    part = rows_dev // cols
    cap = -(-((slots + 1) // 2) * rows_dev // groups)
    me = lax.axis_index("rows")
    here = lax.axis_index("cols")

    def over_rows(x, mask):
        return lax.ppermute(x, "rows", [(i, i ^ mask) for i in range(groups)])

    def over_cols(x, step):
        return lax.ppermute(x, "cols", [(i, (i + step) % cols) for i in range(cols)])

    chips = jnp.concatenate([over_rows(prior, 2 * k) for k in range(1, half)])
    mate = over_rows(prior, 1)
    mate_chips = over_rows(chips, 1)
    early = [prior, chips, mate, mate_chips]

    slot_ids = here * slots + jnp.arange(slots, dtype=I32)
    is_live = slot_ids[None, None, :] < live[:, :, None]
    owner = lax.div(colidx, jnp.int32(prior_dev)) ^ me
    early_at = (
        (owner & 1) * (half * prior_dev)
        + lax.shift_right_logical(owner, jnp.int32(1)) * prior_dev
        + lax.rem(colidx, jnp.int32(prior_dev))
    )
    here_vec = here.astype(I32).reshape(1)
    zero_at = jnp.int32(prior_count)
    first_at = jnp.where(is_live[0], early_at[0], zero_at).reshape(-1)
    own0, msgs0 = partial_products(
        0, cols, jnp.concatenate([first_at, here_vec]), blocks, early
    )

    def find(refs):
        hit = owner_map[0][None, None, :] == (refs - prior_count)[:, :, None]
        ids = jnp.arange(owner_map.shape[1], dtype=I32)
        return jnp.sum(jnp.where(hit, ids[None, None, :], 0), axis=2, dtype=I32)

    flat, msgs0 = lax.optimization_barrier((colidx[1].reshape(1, -1), msgs0))
    near = jnp.concatenate([flat] + [over_rows(flat, 2 * k) for k in range(1, half)])
    refs = jnp.concatenate([near, over_rows(near, 1)])
    order_k = jnp.arange(rows_dev * slots, dtype=I32)
    before = order_k[None, :] < order_k[:, None]
    spots = find(refs)
    mine = (refs >= prior_count) & (lax.div(spots, jnp.int32(rows_dev)) == me)
    rank = jnp.sum(mine[:, None, :] & before[None], axis=2, dtype=I32)
    pick = mine[:, None, :] & (rank[:, None, :] == jnp.arange(cap, dtype=I32)[None, :, None])
    wanted = jnp.sum(
        jnp.where(pick, lax.rem(spots, jnp.int32(rows_dev))[:, None, :], 0), axis=2, dtype=I32
    )

    spot = spots[0]
    is_ref = refs[0] >= prior_count
    holder = lax.div(spot, jnp.int32(rows_dev)) ^ me
    same = (holder[:, None] == holder[None, :]) & is_ref[None, :] & before
    my_rank = jnp.sum(same, axis=1, dtype=I32)
    holder_at = (holder & 1) * half + lax.shift_right_logical(holder, jnp.int32(1))
    recent_at = prior_count + holder_at * cap + my_rank
    second_at = jnp.where(is_ref, recent_at, early_at[1].reshape(-1))
    second_at = jnp.where(is_live[1].reshape(-1), second_at, prior_count + groups * cap)

    rhs_part = lax.dynamic_slice_in_dim(right_side, here * part, part, axis=1)
    inv_part = lax.dynamic_slice_in_dim(diag_inverse, here * part, part, axis=1)

    got0 = [over_cols(m, s + 1) for s, m in enumerate(msgs0)]
    coded0 = solve_part(cols, own0, got0, rhs_part[0], inv_part[0])
    all0 = [coded0] + [over_cols(coded0, s) for s in range(1, cols)]

    first, sends = pack(
        cols,
        groups,
        cap,
        jnp.concatenate([wanted.reshape(-1), here_vec]),
        all0,
        (1,) + right_side.shape[1:],
    )
    masks = [2 * k for k in range(half)] + [2 * k + 1 for k in range(half)]
    recent = [x if m == 0 else over_rows(x, m) for m, x in zip(masks, sends)]

    own1, msgs1 = partial_products(
        1, cols, jnp.concatenate([second_at, here_vec]), blocks, early + recent
    )
    got1 = [over_cols(m, s + 1) for s, m in enumerate(msgs1)]
    coded1 = solve_part(cols, own1, got1, rhs_part[1], inv_part[1])
    all1 = [coded1] + [over_cols(coded1, s) for s in range(1, cols)]
    return last(cols, here_vec, first, all1, right_side.shape)


def solution(mesh):
    placed = (
        P(),
        P(None, "rows", "cols"),
        P(None, "rows"),
        P(None, "rows", "cols", None, None),
        P(None, "rows", None, None),
        P(None, "rows", None, None),
        P("rows", None, None),
    )
    body = functools.partial(shards, mesh.shape["rows"], mesh.shape["cols"])
    return jax.shard_map(
        body, mesh=mesh, in_specs=placed, out_specs=P(None, "rows", None, None), check_vma=False
    )
```

```python
import functools

import jax
import jax.numpy as jnp
from jax import lax
from jax.experimental import pallas as pl
from jax.experimental.pallas import tpu as pltpu
from jax.sharding import PartitionSpec as P

F32, BF16, I32, I16 = jnp.float32, jnp.bfloat16, jnp.int32, jnp.int16
VMEM = pl.BlockSpec(memory_space=pltpu.VMEM)
SMEM = pl.BlockSpec(memory_space=pltpu.SMEM)
HBM = pl.BlockSpec(memory_space=pltpu.HBM)
PARAMS = pltpu.CompilerParams(vmem_limit_bytes=16 * 2**20)
STEPS = 128.0
TAIL = 16
LANES = 128


def encode_blocks(values, msg_ref, probes):
    rows = lax.broadcasted_iota(I32, (TAIL, msg_ref.shape[1]), 0)
    tail = jnp.zeros((TAIL, msg_ref.shape[1]), F32)
    for k, value in enumerate(values):
        peak = jnp.maximum(jnp.max(jnp.abs(value), keepdims=True), 2.0**-100)
        level = jnp.ceil(jnp.log2(peak) * STEPS)
        scaled = jnp.round(value * jnp.exp2(15.0 - level * (1.0 / STEPS)))
        scaled = jnp.clip(scaled, -32767.0, 32767.0)
        msg_ref[k * probes : (k + 1) * probes] = scaled.astype(I32).astype(I16)
        tail = jnp.where(rows == k, level, tail)
    msg_ref[len(values) * probes :] = tail.astype(I32).astype(I16)


def decode_blocks(msg_ref, count, probes):
    tail = msg_ref[count * probes :].astype(I32).astype(F32)
    factor = jnp.exp2(tail * (1.0 / STEPS) - 15.0)
    return [
        msg_ref[k * probes : (k + 1) * probes].astype(I32).astype(F32) * factor[k : k + 1]
        for k in range(count)
    ]


def log2(n):
    return n.bit_length() - 1


def lanes_like(shape, dim):
    return lax.broadcasted_iota(I32, shape, dim)


def table_at(refs, me, prior_dev, half):
    owner = lax.shift_right_logical(refs, log2(prior_dev)) ^ me
    group = (owner & 1) * half + lax.shift_right_logical(owner, 1)
    return group * prior_dev + (refs & (prior_dev - 1))


def spread(values, rows_dev):
    repeat = (lanes_like((rows_dev, LANES), 1) & (rows_dev - 1)) == lanes_like((rows_dev, LANES), 0)
    return jnp.dot(
        values.astype(F32).astype(BF16), repeat.astype(F32).astype(BF16), preferred_element_type=F32
    )


def start_kernel(groups, colidx_ref, live_ref, prior_ref, msg_ref, first_ref, alive_ref, rows):
    slots, _, rows_dev = colidx_ref.shape
    prior_dev, probes, _ = prior_ref.shape
    for k in range(prior_dev):
        msg_ref[k * probes : (k + 1) * probes] = prior_ref[k]
    rows[...] = jnp.zeros(rows.shape, I32)
    for j in range(slots):
        rows[j : j + 1] = colidx_ref[j, 0:1]
        rows[8 + j : 9 + j] = lax.shift_right_logical(colidx_ref[j, 1:2], 4)
        rows[16 + j : 17 + j] = colidx_ref[j, 1:2] & 15
        rows[24 + j : 25 + j] = lax.shift_right_logical(colidx_ref[j, 0:1], 4)
        rows[32 + j : 33 + j] = colidx_ref[j, 0:1] & 15
    rows[40:42] = live_ref[...]
    wide = spread(rows[...], rows_dev)
    msg_ref[prior_dev * probes :] = wide[8:24].astype(BF16)
    me, here = lax.axis_index("rows"), lax.axis_index("cols")
    ids = here * slots + lanes_like((8, LANES), 0)
    refs = (wide[24:32] * 16.0 + wide[32:40]).astype(I32)
    live = wide[40:48].astype(I32)
    found = table_at(refs, me, prior_dev, groups // 2)
    first_ref[...] = jnp.where(ids < live[0:1], found, groups * prior_dev)
    alive_ref[...] = (ids < live[1:2]).astype(I32)


def start(groups, colidx, live, prior):
    rows_dev, slots = colidx.shape[1:]
    prior_dev, probes, order = prior.shape
    table = jax.ShapeDtypeStruct((8, LANES), I32)
    return pl.pallas_call(
        functools.partial(start_kernel, groups),
        out_shape=[jax.ShapeDtypeStruct((prior_dev * probes + TAIL, order), BF16), table, table],
        in_specs=[VMEM] * 3,
        out_specs=[VMEM] * 3,
        scratch_shapes=[pltpu.VMEM((48, rows_dev), I32)],
        compiler_params=PARAMS,
        name="start",
    )(jnp.transpose(colidx, (2, 0, 1)), live, prior)


def ranks(mask, within, slots):
    ones = mask.astype(F32).astype(BF16)
    before = jnp.dot(ones, within[0], preferred_element_type=F32)
    count = jnp.dot(ones, within[1], preferred_element_type=F32)
    above = jnp.zeros((1, LANES), F32)
    rows = lanes_like((8, LANES), 0)
    for j in range(slots):
        before = jnp.where(rows == j, before + above, before)
        above = above + count[j : j + 1]
    return before


def route_kernel(groups, cap, slots, prior_dev, owner_ref, alive_ref, *refs):
    tails, want_ref, second_ref = refs[:groups], refs[groups], refs[groups + 1]
    rows_front = owner_ref.shape[1]
    rows_dev = rows_front // groups
    half = groups // 2
    prior_count = groups * prior_dev
    me = lax.axis_index("rows")
    per = LANES // rows_dev
    lane = lanes_like((8, LANES), 1)
    group_of = lax.shift_right_logical(lane, log2(rows_dev))
    a, b = lanes_like((LANES, LANES), 0), lanes_like((LANES, LANES), 1)
    together = lax.shift_right_logical(a, log2(rows_dev)) == lax.shift_right_logical(b, log2(rows_dev))
    alike = (a & (rows_dev - 1)) == (b & (rows_dev - 1))
    as_bf16 = lambda x: x.astype(F32).astype(BF16)
    within = (as_bf16(together & (a < b)), as_bf16(together))

    def referred(g):
        tail = tails[g][tails[g].shape[0] - TAIL :].astype(F32)
        return (tail[:8] * 16.0 + tail[8:]).astype(I32)

    want_ref[...] = jnp.zeros(want_ref.shape, I32)
    for block in range(groups // per):
        named = referred(block * per)
        for g in range(1, per):
            named = jnp.where(group_of == g, referred(block * per + g), named)
        spot = jnp.full((8, LANES), -1, I32)
        for t in range(rows_dev):
            spot = jnp.where(named == prior_count + owner_ref[0, me * rows_dev + t], t, spot)
        mine = spot >= 0
        rank = ranks(mine, within, slots).astype(I32)
        for q in range(cap):
            held = jnp.where(mine & (rank == q), spot, 0).astype(F32).astype(BF16)
            total = jnp.dot(held, within[1], preferred_element_type=F32)
            want_ref[q : q + 1, block * LANES : (block + 1) * LANES] = jnp.sum(
                total, axis=0, keepdims=True
            ).astype(I32)

    own = referred(0)
    recent = own >= prior_count
    spot = jnp.zeros((8, LANES), I32)
    for t in range(rows_front):
        spot = jnp.where(own == prior_count + owner_ref[0, t], t, spot)
    holder = lax.shift_right_logical(spot, log2(rows_dev)) ^ me
    group = (holder & 1) * half + lax.shift_right_logical(holder, 1)
    rank = jnp.zeros((8, LANES), F32)
    for block in range(groups // per):
        mask = recent & (group == group_of + block * per)
        found = jnp.where(mask, ranks(mask, within, slots), 0.0)
        rank = rank + jnp.dot(found.astype(BF16), as_bf16(alike), preferred_element_type=F32)
    at = jnp.where(
        recent,
        prior_count + group * cap + rank.astype(I32),
        table_at(own, me, prior_dev, half),
    )
    second_ref[...] = jnp.where(alive_ref[...] > 0, at, prior_count + groups * cap)


def route(groups, cap, slots, prior_dev, owner_map, alive, pieces):
    rows_dev = owner_map.shape[1] // groups
    return pl.pallas_call(
        functools.partial(route_kernel, groups, cap, slots, prior_dev),
        out_shape=[
            jax.ShapeDtypeStruct((-(-cap // 8) * 8, groups * rows_dev), I32),
            jax.ShapeDtypeStruct((8, LANES), I32),
        ],
        in_specs=[SMEM] + [VMEM] * (groups + 1),
        out_specs=[VMEM] * 2,
        compiler_params=PARAMS,
        name="route",
    )(owner_map, alive, *pieces)


def load_kernel(blocks, right_side, inverse, *refs):
    outs, sems = refs[:-1], refs[-1]
    part = outs[2].shape[1]
    first = lax.axis_index("cols") * part
    sources = [
        blocks.at[0],
        blocks.at[1],
        right_side.at[:, pl.ds(first, part)],
        inverse.at[:, pl.ds(first, part)],
    ]
    copies = [pltpu.make_async_copy(a, b, sems.at[i]) for i, (a, b) in enumerate(zip(sources, outs))]
    for copy in copies:
        copy.start()
    for copy in copies:
        copy.wait()


def load(cols, blocks, right_side, inverse):
    part = blocks.shape[1] // cols
    shapes = [blocks.shape[1:]] * 2
    shapes += [a.shape[:1] + (part,) + a.shape[2:] for a in (right_side, inverse)]
    kinds = [BF16, BF16, F32, F32]
    return pl.pallas_call(
        load_kernel,
        out_shape=[pltpu.VMEM(a, b) for a, b in zip(shapes, kinds)],
        in_specs=[HBM] * 3,
        out_specs=[VMEM] * 4,
        scratch_shapes=[pltpu.SemaphoreType.DMA((4,))],
        compiler_params=PARAMS,
        name="load",
    )(*(pltpu.with_memory_space_constraint(x, pltpu.HBM) for x in (blocks, right_side, inverse)))


def partial_kernel(cols, n_early, probes, idx_ref, blk, *refs):
    ins, own_ref, msgs, known = refs[:-cols - 1], refs[-cols - 1], refs[-cols:-1], refs[-1]
    rows_dev, slots, order, _ = blk.shape
    part = rows_dev // cols
    here = lax.axis_index("cols")
    at = 0
    for i, ref in enumerate(ins):
        for k in range((ref.shape[0] - (TAIL if i < n_early else 0)) // probes):
            known[at] = ref[k * probes : (k + 1) * probes]
            at += 1
    known[at] = jnp.zeros(known.shape[1:], known.dtype)
    for s in list(range(1, cols)) + [0]:
        first = lax.rem(here + s, cols) * part
        sums = []
        for k in range(part):
            xs = [known[idx_ref[j, first + k]] for j in range(slots)]
            ws = [blk[first + k, j] for j in range(slots)]
            sums.append(
                lax.dot_general(
                    jnp.concatenate(xs, axis=1),
                    jnp.concatenate(ws, axis=1),
                    (((1,), (1,)), ((), ())),
                    preferred_element_type=F32,
                )
            )
        if s == 0:
            for k in range(part):
                own_ref[k] = sums[k]
        else:
            encode_blocks(sums, msgs[s - 1], probes)


def partial_products(name, cols, probes, idx, blocks, early, recent):
    rows_dev, slots, order, _ = blocks.shape
    part = rows_dev // cols
    rows = sum(a.shape[0] - TAIL for a in early) + sum(a.shape[0] for a in recent)
    msg = jax.ShapeDtypeStruct((part * probes + TAIL, order), I16)
    out = pl.pallas_call(
        functools.partial(partial_kernel, cols, len(early), probes),
        out_shape=[jax.ShapeDtypeStruct((part, probes, order), F32)] + [msg] * (cols - 1),
        in_specs=[SMEM] + [VMEM] * (len(early) + len(recent) + 1),
        out_specs=[VMEM] * cols,
        scratch_shapes=[pltpu.VMEM((rows // probes + 1, probes, order), BF16)],
        compiler_params=PARAMS,
        name=name,
    )(idx, blocks, *early, *recent)
    return out[0], out[1:]


def solve_kernel(front, cols, own_ref, *refs):
    msgs, rhs_ref, inv_ref, out_ref = refs[: cols - 1], refs[cols - 1], refs[cols], refs[cols + 1]
    part, probes, _ = own_ref.shape
    total = [own_ref[k] for k in range(part)]
    for msg in msgs:
        total = [a + b for a, b in zip(total, decode_blocks(msg, part, probes))]
    solved = [
        lax.dot_general(
            rhs_ref[front, k] - total[k],
            inv_ref[front, k],
            (((1,), (1,)), ((), ())),
            precision=lax.Precision.HIGHEST,
            preferred_element_type=F32,
        )
        for k in range(part)
    ]
    encode_blocks(solved, out_ref, probes)


def solve_part(front, cols, own, msgs, rhs, inverse):
    part, probes, order = own.shape
    return pl.pallas_call(
        functools.partial(solve_kernel, front, cols),
        out_shape=jax.ShapeDtypeStruct((part * probes + TAIL, order), I16),
        in_specs=[VMEM] * (cols + 2),
        out_specs=VMEM,
        compiler_params=PARAMS,
        name=f"solve_{front}",
    )(own, *msgs, rhs, inverse)


def pack_kernel(cols, groups, cap, sel_ref, *refs):
    msgs, sends, rows = refs[:cols], refs[cols:-1], refs[-1]
    rows_dev, probes, _ = rows.shape
    part = rows_dev // cols
    here = lax.axis_index("cols")
    for s in range(cols):
        first = lax.rem(here + cols - s, cols) * part
        for k, value in enumerate(decode_blocks(msgs[s], part, probes)):
            rows[first + k] = value.astype(BF16)
    for m in range(groups):
        for q in range(cap):
            sends[m][q * probes : (q + 1) * probes] = rows[sel_ref[q, m * rows_dev]]


def pack(cols, groups, cap, sel, msgs, shape):
    rows_dev, probes, order = shape
    return pl.pallas_call(
        functools.partial(pack_kernel, cols, groups, cap),
        out_shape=[jax.ShapeDtypeStruct((cap * probes, order), BF16)] * groups,
        in_specs=[SMEM] + [VMEM] * cols,
        out_specs=[VMEM] * groups,
        scratch_shapes=[pltpu.VMEM((rows_dev, probes, order), BF16)],
        compiler_params=PARAMS,
        name="pack",
    )(sel, *msgs)


def unpack_kernel(front, cols, *refs):
    msgs, out_ref, rows, sems = refs[:cols], refs[-3], refs[-2], refs[-1]
    part, probes, _ = rows.shape[1:]
    here = lax.axis_index("cols")
    copies = []
    for s in range(cols):
        first = lax.rem(here + cols - s, cols) * part
        for k, value in enumerate(decode_blocks(msgs[s], part, probes)):
            rows[s, k] = value
        copy = pltpu.make_async_copy(rows.at[s], out_ref.at[front, pl.ds(first, part)], sems.at[s])
        copy.start()
        copies.append(copy)
    for copy in copies:
        copy.wait()


def unpack(front, cols, msgs, shape, base=None):
    _, rows_dev, probes, order = shape
    rest = [] if base is None else [base]
    return pl.pallas_call(
        functools.partial(unpack_kernel, front, cols),
        out_shape=jax.ShapeDtypeStruct(shape, F32),
        in_specs=[VMEM] * cols + [HBM] * len(rest),
        out_specs=HBM,
        input_output_aliases={} if base is None else {cols: 0},
        scratch_shapes=[
            pltpu.VMEM((cols, rows_dev // cols, probes, order), F32),
            pltpu.SemaphoreType.DMA((cols,)),
        ],
        compiler_params=PARAMS,
        name=f"unpack_{front}",
    )(*msgs, *rest)


def shards(groups, cols, owner_map, colidx, live, blocks, diag_inverse, right_side, prior):
    _, rows_dev, slots, order, _ = blocks.shape
    probes = right_side.shape[2]
    prior_dev = prior.shape[0]
    half = groups // 2
    cap = -(-((slots + 1) // 2) * rows_dev // groups)
    def over_rows(x, mask):
        return lax.ppermute(x, "rows", [(i, i ^ mask) for i in range(groups)])

    def over_cols(x, step):
        return lax.ppermute(x, "cols", [(i, (i + step) % cols) for i in range(cols)])

    own, first_at, alive = start(groups, colidx, live, prior)
    pieces = [own] + [over_rows(own, 2 * k) for k in range(1, half)]
    pieces += [over_rows(x, 1) for x in pieces]
    blocks0, blocks1, rhs, inverse = load(cols, blocks, right_side, diag_inverse)
    want, second_at = route(groups, cap, slots, prior_dev, owner_map, alive, pieces)

    own0, msgs0 = partial_products("partial_0", cols, probes, first_at, blocks0, pieces, [])
    got0 = [over_cols(m, s + 1) for s, m in enumerate(msgs0)]
    coded0 = solve_part(0, cols, own0, got0, rhs, inverse)
    all0 = [coded0] + [over_cols(coded0, s) for s in range(1, cols)]

    sends = pack(cols, groups, cap, want, all0, right_side.shape[1:])
    masks = [2 * k for k in range(half)] + [2 * k + 1 for k in range(half)]
    recent = [x if m == 0 else over_rows(x, m) for m, x in zip(masks, sends)]
    solved = unpack(0, cols, all0, right_side.shape)

    own1, msgs1 = partial_products("partial_1", cols, probes, second_at, blocks1, pieces, recent)
    got1 = [over_cols(m, s + 1) for s, m in enumerate(msgs1)]
    coded1 = solve_part(1, cols, own1, got1, rhs, inverse)
    all1 = [coded1] + [over_cols(coded1, s) for s in range(1, cols)]
    return unpack(1, cols, all1, right_side.shape, solved)


def solution(mesh):
    placed = (
        P(),
        P(None, "rows", "cols"),
        P(None, "rows"),
        P(None, "rows", "cols", None, None),
        P(None, "rows", None, None),
        P(None, "rows", None, None),
        P("rows", None, None),
    )
    body = functools.partial(shards, mesh.shape["rows"], mesh.shape["cols"])
    return jax.shard_map(
        body, mesh=mesh, in_specs=placed, out_specs=P(None, "rows", None, None), check_vma=False
    )
```

```python
import functools

import jax
import jax.numpy as jnp
from jax import lax
from jax.experimental import pallas as pl
from jax.experimental.pallas import tpu as pltpu
from jax.sharding import PartitionSpec as P

F32, BF16, I32, I16 = jnp.float32, jnp.bfloat16, jnp.int32, jnp.int16
VMEM = pl.BlockSpec(memory_space=pltpu.VMEM)
SMEM = pl.BlockSpec(memory_space=pltpu.SMEM)
HBM = pl.BlockSpec(memory_space=pltpu.HBM)
PARAMS = pltpu.CompilerParams(vmem_limit_bytes=16 * 2**20)
STEPS = 128.0
TAIL = 16
LANES = 128


def encode_blocks(values, msg_ref, probes):
    rows = lax.broadcasted_iota(I32, (TAIL, msg_ref.shape[1]), 0)
    tail = jnp.zeros((TAIL, msg_ref.shape[1]), F32)
    for k, value in enumerate(values):
        peak = jnp.maximum(jnp.max(jnp.abs(value), keepdims=True), 2.0**-100)
        level = jnp.ceil(jnp.log2(peak) * STEPS)
        scaled = jnp.round(value * jnp.exp2(15.0 - level * (1.0 / STEPS)))
        scaled = jnp.clip(scaled, -32767.0, 32767.0)
        msg_ref[k * probes : (k + 1) * probes] = scaled.astype(I32).astype(I16)
        tail = jnp.where(rows == k, level, tail)
    msg_ref[len(values) * probes :] = tail.astype(I32).astype(I16)


def decode_blocks(msg_ref, count, probes):
    tail = msg_ref[count * probes :].astype(I32).astype(F32)
    factor = jnp.exp2(tail * (1.0 / STEPS) - 15.0)
    return [
        msg_ref[k * probes : (k + 1) * probes].astype(I32).astype(F32) * factor[k : k + 1]
        for k in range(count)
    ]


def in_hbm(x):
    return pltpu.with_memory_space_constraint(x, pltpu.HBM)


def in_smem(x):
    return pltpu.with_memory_space_constraint(x, pltpu.SMEM)


def log2(n):
    return n.bit_length() - 1


def lanes_like(shape, dim):
    return lax.broadcasted_iota(I32, shape, dim)


def table_at(refs, me, prior_dev, half):
    owner = lax.shift_right_logical(refs, log2(prior_dev)) ^ me
    group = (owner & 1) * half + lax.shift_right_logical(owner, 1)
    return group * prior_dev + (refs & (prior_dev - 1))


def spread(values, rows_dev):
    repeat = (lanes_like((rows_dev, LANES), 1) & (rows_dev - 1)) == lanes_like((rows_dev, LANES), 0)
    return jnp.dot(
        values.astype(F32).astype(BF16), repeat.astype(F32).astype(BF16), preferred_element_type=F32
    )


def start_kernel(groups, prior_dev, colidx, live, prior, msg_ref, first_ref, alive_ref, *scratch):
    colidx_ref, live_ref, rows, sems = scratch
    slots, _, rows_dev = colidx_ref.shape
    copies = [
        pltpu.make_async_copy(prior, msg_ref.at[pl.ds(0, prior.shape[0])], sems.at[0]),
        pltpu.make_async_copy(colidx, colidx_ref, sems.at[1]),
        pltpu.make_async_copy(live, live_ref, sems.at[2]),
    ]
    for copy in copies:
        copy.start()
    rows[...] = jnp.zeros(rows.shape, I32)
    copies[1].wait()
    copies[2].wait()
    for j in range(slots):
        rows[j : j + 1] = colidx_ref[j, 0:1]
        rows[8 + j : 9 + j] = lax.shift_right_logical(colidx_ref[j, 1:2], 4)
        rows[16 + j : 17 + j] = colidx_ref[j, 1:2] & 15
        rows[24 + j : 25 + j] = lax.shift_right_logical(colidx_ref[j, 0:1], 4)
        rows[32 + j : 33 + j] = colidx_ref[j, 0:1] & 15
    rows[40:42] = live_ref[...]
    wide = spread(rows[...], rows_dev)
    msg_ref[prior.shape[0] :] = wide[8:24].astype(BF16)
    me, here = lax.axis_index("rows"), lax.axis_index("cols")
    ids = here * slots + lanes_like((8, LANES), 0)
    refs = (wide[24:32] * 16.0 + wide[32:40]).astype(I32)
    live = wide[40:48].astype(I32)
    found = table_at(refs, me, prior_dev, groups // 2)
    first_ref[...] = jnp.where(ids < live[0:1], found, groups * prior_dev)
    alive_ref[...] = (ids < live[1:2]).astype(I32)
    copies[0].wait()


def start(groups, colidx, live, prior):
    rows_dev, slots = colidx.shape[1:]
    prior_dev, probes, order = prior.shape
    table = jax.ShapeDtypeStruct((8, LANES), I32)
    return pl.pallas_call(
        functools.partial(start_kernel, groups, prior_dev),
        out_shape=[jax.ShapeDtypeStruct((prior_dev * probes + TAIL, order), BF16), table, table],
        in_specs=[HBM] * 3,
        out_specs=[VMEM] * 3,
        scratch_shapes=[
            pltpu.VMEM((slots, 2, rows_dev), I32),
            pltpu.VMEM((2, rows_dev), I32),
            pltpu.VMEM((48, rows_dev), I32),
            pltpu.SemaphoreType.DMA((3,)),
        ],
        compiler_params=PARAMS,
        name="start",
    )(*(in_hbm(x) for x in (jnp.transpose(colidx, (2, 0, 1)), live, prior.reshape(-1, order))))


def ranks(mask, within, slots):
    ones = mask.astype(F32).astype(BF16)
    before = jnp.dot(ones, within[0], preferred_element_type=F32)
    count = jnp.dot(ones, within[1], preferred_element_type=F32)
    above = jnp.zeros((1, LANES), F32)
    rows = lanes_like((8, LANES), 0)
    for j in range(slots):
        before = jnp.where(rows == j, before + above, before)
        above = above + count[j : j + 1]
    return before


def route_kernel(groups, cap, slots, prior_dev, owner_ref, alive_ref, *refs):
    tails, outs = refs[:groups], refs[groups : groups + 2]
    want_ref, second_ref, sems = refs[groups + 2 :]
    rows_front = owner_ref.shape[1]
    rows_dev = rows_front // groups
    half = groups // 2
    prior_count = groups * prior_dev
    me = lax.axis_index("rows")
    per = LANES // rows_dev
    lane = lanes_like((8, LANES), 1)
    group_of = lax.shift_right_logical(lane, log2(rows_dev))
    a, b = lanes_like((LANES, LANES), 0), lanes_like((LANES, LANES), 1)
    together = lax.shift_right_logical(a, log2(rows_dev)) == lax.shift_right_logical(b, log2(rows_dev))
    alike = (a & (rows_dev - 1)) == (b & (rows_dev - 1))
    as_bf16 = lambda x: x.astype(F32).astype(BF16)
    within = (as_bf16(together & (a < b)), as_bf16(together))

    def referred(g):
        tail = tails[g][tails[g].shape[0] - TAIL :].astype(F32)
        return (tail[:8] * 16.0 + tail[8:]).astype(I32)

    want_ref[...] = jnp.zeros(want_ref.shape, I32)
    for block in range(groups // per):
        named = referred(block * per)
        for g in range(1, per):
            named = jnp.where(group_of == g, referred(block * per + g), named)
        spot = jnp.full((8, LANES), -1, I32)
        for t in range(rows_dev):
            spot = jnp.where(named == prior_count + owner_ref[0, me * rows_dev + t], t, spot)
        mine = spot >= 0
        rank = ranks(mine, within, slots).astype(I32)
        for q in range(cap):
            held = jnp.where(mine & (rank == q), spot, 0).astype(F32).astype(BF16)
            total = jnp.dot(held, within[1], preferred_element_type=F32)
            want_ref[q : q + 1, block * LANES : (block + 1) * LANES] = jnp.sum(
                total, axis=0, keepdims=True
            ).astype(I32)

    own = referred(0)
    recent = own >= prior_count
    spot = jnp.zeros((8, LANES), I32)
    for t in range(rows_front):
        spot = jnp.where(own == prior_count + owner_ref[0, t], t, spot)
    holder = lax.shift_right_logical(spot, log2(rows_dev)) ^ me
    group = (holder & 1) * half + lax.shift_right_logical(holder, 1)
    rank = jnp.zeros((8, LANES), F32)
    for block in range(groups // per):
        mask = recent & (group == group_of + block * per)
        found = jnp.where(mask, ranks(mask, within, slots), 0.0)
        rank = rank + jnp.dot(found.astype(BF16), as_bf16(alike), preferred_element_type=F32)
    at = jnp.where(
        recent,
        prior_count + group * cap + rank.astype(I32),
        table_at(own, me, prior_dev, half),
    )
    second_ref[...] = jnp.where(alive_ref[...] > 0, at, prior_count + groups * cap)
    copies = [
        pltpu.make_async_copy(x, out, sems.at[i])
        for i, (x, out) in enumerate(zip((want_ref, second_ref), outs))
    ]
    for copy in copies:
        copy.start()
    for copy in copies:
        copy.wait()


def route(groups, cap, slots, prior_dev, owner_map, alive, pieces):
    shapes = [(-(-cap // 8) * 8, owner_map.shape[1]), (8, LANES)]
    return pl.pallas_call(
        functools.partial(route_kernel, groups, cap, slots, prior_dev),
        out_shape=[pltpu.SMEM(a, I32) for a in shapes],
        in_specs=[SMEM] + [VMEM] * (groups + 1),
        out_specs=[SMEM] * 2,
        scratch_shapes=[pltpu.VMEM(a, I32) for a in shapes] + [pltpu.SemaphoreType.DMA((2,))],
        compiler_params=PARAMS,
        name="route",
    )(owner_map, alive, *pieces)


def load_kernel(cols, first_at, blocks, right_side, inverse, *refs):
    outs, at_ref, raw, raw_inverse, sems = refs[:4], refs[4], refs[5], refs[6], refs[7]
    fronts, rows_dev, slots = blocks.shape[:3]
    part = rows_dev // cols
    first = lax.axis_index("cols") * part
    names = pltpu.make_async_copy(first_at, at_ref, sems.at[fronts * cols + 2])
    names.start()
    copies = []
    for f in range(fronts):
        for s in range(cols):
            rows = pl.ds(s * part, part)
            copies.append(
                pltpu.make_async_copy(
                    blocks.at[f, rows], raw.at[f, rows], sems.at[f * cols + s]
                )
            )
    copies += [
        pltpu.make_async_copy(
            inverse.at[:, pl.ds(first, part)], raw_inverse, sems.at[fronts * cols]
        ),
        pltpu.make_async_copy(
            right_side.at[:, pl.ds(first, part)], outs[2], sems.at[fronts * cols + 1]
        ),
    ]
    for copy in copies:
        copy.start()
    for f in range(fronts):
        for s in range(cols):
            copies[f * cols + s].wait()
            for i in range(s * part, (s + 1) * part):
                for j in range(slots):
                    outs[f][i, j] = raw[f, i, j].T
    copies[-2].wait()
    for f in range(fronts):
        for k in range(part):
            outs[3][f, k] = raw_inverse[f, k].T
    copies[-1].wait()
    names.wait()


def load(cols, first_at, blocks, right_side, inverse):
    part = blocks.shape[1] // cols
    shapes = [blocks.shape[1:]] * 2
    shapes += [a.shape[:1] + (part,) + a.shape[2:] for a in (right_side, inverse)]
    kinds = [BF16, BF16, F32, F32]
    return pl.pallas_call(
        functools.partial(load_kernel, cols),
        out_shape=[pltpu.VMEM(a, b) for a, b in zip(shapes, kinds)]
        + [pltpu.SMEM(first_at.shape, I32)],
        in_specs=[VMEM] + [HBM] * 3,
        out_specs=[VMEM] * 4 + [SMEM],
        scratch_shapes=[
            pltpu.VMEM(blocks.shape, BF16),
            pltpu.VMEM(shapes[3], F32),
            pltpu.SemaphoreType.DMA((2 * cols + 3,)),
        ],
        compiler_params=PARAMS,
        cost_estimate=pl.CostEstimate(
            flops=0, transcendentals=0, bytes_accessed=2 * blocks.size * blocks.dtype.itemsize
        ),
        name="load",
    )(first_at, *(in_hbm(x) for x in (blocks, right_side, inverse)))


def partial_kernel(cols, n_early, probes, idx_ref, blk, *refs):
    ins, own_ref, msgs, known = refs[:-cols - 1], refs[-cols - 1], refs[-cols:-1], refs[-1]
    rows_dev, slots, order, _ = blk.shape
    part = rows_dev // cols
    here = lax.axis_index("cols")
    at = 0
    for i, ref in enumerate(ins):
        for k in range((ref.shape[0] - (TAIL if i < n_early else 0)) // probes):
            known[at] = ref[k * probes : (k + 1) * probes]
            at += 1
    known[at] = jnp.zeros(known.shape[1:], known.dtype)
    for s in list(range(1, cols)) + [0]:
        first = lax.rem(here + s, cols) * part
        sums = []
        for k in range(part):
            xs = [known[idx_ref[j, first + k]] for j in range(slots)]
            ws = [blk[first + k, j] for j in range(slots)]
            sums.append(
                lax.dot_general(
                    jnp.concatenate(xs, axis=1),
                    jnp.concatenate(ws, axis=0),
                    (((1,), (0,)), ((), ())),
                    preferred_element_type=F32,
                )
            )
        if s == 0:
            for k in range(part):
                own_ref[k] = sums[k]
        else:
            encode_blocks(sums, msgs[s - 1], probes)


def partial_products(name, cols, probes, idx, blocks, early, recent):
    rows_dev, slots, order, _ = blocks.shape
    part = rows_dev // cols
    rows = sum(a.shape[0] - TAIL for a in early) + sum(a.shape[0] for a in recent)
    msg = jax.ShapeDtypeStruct((part * probes + TAIL, order), I16)
    out = pl.pallas_call(
        functools.partial(partial_kernel, cols, len(early), probes),
        out_shape=[jax.ShapeDtypeStruct((part, probes, order), F32)] + [msg] * (cols - 1),
        in_specs=[SMEM] + [VMEM] * (len(early) + len(recent) + 1),
        out_specs=[VMEM] * cols,
        scratch_shapes=[pltpu.VMEM((rows // probes + 1, probes, order), BF16)],
        compiler_params=PARAMS,
        name=name,
    )(in_smem(idx), blocks, *early, *recent)
    return out[0], out[1:]


def solve_kernel(front, cols, own_ref, *refs):
    msgs, rhs_ref, inv_ref, out_ref = refs[: cols - 1], refs[cols - 1], refs[cols], refs[cols + 1]
    part, probes, _ = own_ref.shape
    total = [own_ref[k] for k in range(part)]
    for msg in msgs:
        total = [a + b for a, b in zip(total, decode_blocks(msg, part, probes))]
    solved = [
        lax.dot_general(
            rhs_ref[front, k] - total[k],
            inv_ref[front, k],
            (((1,), (0,)), ((), ())),
            precision=lax.Precision.HIGHEST,
            preferred_element_type=F32,
        )
        for k in range(part)
    ]
    encode_blocks(solved, out_ref, probes)


def solve_part(front, cols, own, msgs, rhs, inverse):
    part, probes, order = own.shape
    return pl.pallas_call(
        functools.partial(solve_kernel, front, cols),
        out_shape=jax.ShapeDtypeStruct((part * probes + TAIL, order), I16),
        in_specs=[VMEM] * (cols + 2),
        out_specs=VMEM,
        compiler_params=PARAMS,
        name=f"solve_{front}",
    )(own, *msgs, rhs, inverse)


def pack_kernel(cols, groups, cap, sel_ref, *refs):
    msgs, sends, rows = refs[:cols], refs[cols:-1], refs[-1]
    rows_dev, probes, _ = rows.shape
    part = rows_dev // cols
    here = lax.axis_index("cols")
    for s in range(cols):
        first = lax.rem(here + cols - s, cols) * part
        for k, value in enumerate(decode_blocks(msgs[s], part, probes)):
            rows[first + k] = value.astype(BF16)
    for m in range(groups):
        for q in range(cap):
            sends[m][q * probes : (q + 1) * probes] = rows[sel_ref[q, m * rows_dev]]


def pack(cols, groups, cap, sel, msgs, shape):
    rows_dev, probes, order = shape
    return pl.pallas_call(
        functools.partial(pack_kernel, cols, groups, cap),
        out_shape=[jax.ShapeDtypeStruct((cap * probes, order), BF16)] * groups,
        in_specs=[SMEM] + [VMEM] * cols,
        out_specs=[VMEM] * groups,
        scratch_shapes=[pltpu.VMEM((rows_dev, probes, order), BF16)],
        compiler_params=PARAMS,
        name="pack",
    )(in_smem(sel), *msgs)


def unpack_kernel(front, cols, *refs):
    msgs, out_ref, rows, sems = refs[:cols], refs[-3], refs[-2], refs[-1]
    part, probes, _ = rows.shape[1:]
    here = lax.axis_index("cols")
    copies = []
    for s in range(cols):
        first = lax.rem(here + cols - s, cols) * part
        for k, value in enumerate(decode_blocks(msgs[s], part, probes)):
            rows[s, k] = value
        copy = pltpu.make_async_copy(rows.at[s], out_ref.at[front, pl.ds(first, part)], sems.at[s])
        copy.start()
        copies.append(copy)
    for copy in copies:
        copy.wait()


def unpack(front, cols, msgs, shape, base=None):
    _, rows_dev, probes, order = shape
    rest = [] if base is None else [base]
    return pl.pallas_call(
        functools.partial(unpack_kernel, front, cols),
        out_shape=jax.ShapeDtypeStruct(shape, F32),
        in_specs=[VMEM] * cols + [HBM] * len(rest),
        out_specs=HBM,
        input_output_aliases={} if base is None else {cols: 0},
        scratch_shapes=[
            pltpu.VMEM((cols, rows_dev // cols, probes, order), F32),
            pltpu.SemaphoreType.DMA((cols,)),
        ],
        compiler_params=PARAMS,
        name=f"unpack_{front}",
    )(*msgs, *rest)


def shards(groups, cols, owner_map, colidx, live, blocks, diag_inverse, right_side, prior):
    _, rows_dev, slots, order, _ = blocks.shape
    probes = right_side.shape[2]
    prior_dev = prior.shape[0]
    half = groups // 2
    cap = -(-((slots + 1) // 2) * rows_dev // groups)
    def over_rows(x, mask):
        return lax.ppermute(x, "rows", [(i, i ^ mask) for i in range(groups)])

    def over_cols(x, step):
        return lax.ppermute(x, "cols", [(i, (i + step) % cols) for i in range(cols)])

    own, first_at, alive = start(groups, colidx, live, prior)
    chips = [over_rows(own, 2 * k) for k in range(1, half)]
    blocks0, blocks1, rhs, inverse, first_at = load(
        cols, first_at, blocks, right_side, diag_inverse
    )
    chips, blocks0 = lax.optimization_barrier((chips, blocks0))
    pieces = [own] + chips
    pieces += [over_rows(x, 1) for x in pieces]
    want, second_at = route(groups, cap, slots, prior_dev, owner_map, alive, pieces)

    own0, msgs0 = partial_products("partial_0", cols, probes, first_at, blocks0, pieces, [])
    got0 = [over_cols(m, s + 1) for s, m in enumerate(msgs0)]
    coded0 = solve_part(0, cols, own0, got0, rhs, inverse)
    all0 = [coded0] + [over_cols(coded0, s) for s in range(1, cols)]

    sends = pack(cols, groups, cap, want, all0, right_side.shape[1:])
    masks = [2 * k for k in range(half)] + [2 * k + 1 for k in range(half)]
    recent = [x if m == 0 else over_rows(x, m) for m, x in zip(masks, sends)]
    solved = unpack(0, cols, all0, right_side.shape)

    own1, msgs1 = partial_products("partial_1", cols, probes, second_at, blocks1, pieces, recent)
    got1 = [over_cols(m, s + 1) for s, m in enumerate(msgs1)]
    coded1 = solve_part(1, cols, own1, got1, rhs, inverse)
    all1 = [coded1] + [over_cols(coded1, s) for s in range(1, cols)]
    return unpack(1, cols, all1, right_side.shape, solved)


def solution(mesh):
    placed = (
        P(),
        P(None, "rows", "cols"),
        P(None, "rows"),
        P(None, "rows", "cols", None, None),
        P(None, "rows", None, None),
        P(None, "rows", None, None),
        P("rows", None, None),
    )
    body = functools.partial(shards, mesh.shape["rows"], mesh.shape["cols"])
    return jax.shard_map(
        body, mesh=mesh, in_specs=placed, out_specs=P(None, "rows", None, None), check_vma=False
    )
```

```python
import functools

import jax
import jax.numpy as jnp
from jax import lax
from jax.experimental import pallas as pl
from jax.experimental.pallas import tpu as pltpu
from jax.sharding import PartitionSpec as P

F32, BF16, I32, I16 = jnp.float32, jnp.bfloat16, jnp.int32, jnp.int16
VMEM = pl.BlockSpec(memory_space=pltpu.VMEM)
SMEM = pl.BlockSpec(memory_space=pltpu.SMEM)
HBM = pl.BlockSpec(memory_space=pltpu.HBM)
PARAMS = pltpu.CompilerParams(vmem_limit_bytes=16 * 2**20)
STEPS = 128.0
TAIL = 16
LANES = 128


def encode_blocks(values, msg_ref, probes):
    rows = lax.broadcasted_iota(I32, (TAIL, msg_ref.shape[1]), 0)
    tail = jnp.zeros((TAIL, msg_ref.shape[1]), F32)
    for k, value in enumerate(values):
        peak = jnp.maximum(jnp.max(jnp.abs(value), keepdims=True), 2.0**-100)
        level = jnp.ceil(jnp.log2(peak) * STEPS)
        scaled = jnp.round(value * jnp.exp2(15.0 - level * (1.0 / STEPS)))
        scaled = jnp.clip(scaled, -32767.0, 32767.0)
        msg_ref[k * probes : (k + 1) * probes] = scaled.astype(I32).astype(I16)
        tail = jnp.where(rows == k, level, tail)
    msg_ref[len(values) * probes :] = tail.astype(I32).astype(I16)


def decode_blocks(msg_ref, count, probes):
    tail = msg_ref[count * probes :].astype(I32).astype(F32)
    factor = jnp.exp2(tail * (1.0 / STEPS) - 15.0)
    return [
        msg_ref[k * probes : (k + 1) * probes].astype(I32).astype(F32) * factor[k : k + 1]
        for k in range(count)
    ]


def in_hbm(x):
    return pltpu.with_memory_space_constraint(x, pltpu.HBM)


def in_smem(x):
    return pltpu.with_memory_space_constraint(x, pltpu.SMEM)


def log2(n):
    return n.bit_length() - 1


def lanes_like(shape, dim):
    return lax.broadcasted_iota(I32, shape, dim)


def table_at(refs, me, prior_dev, half):
    owner = lax.shift_right_logical(refs, log2(prior_dev)) ^ me
    group = (owner & 1) * half + lax.shift_right_logical(owner, 1)
    return group * prior_dev + (refs & (prior_dev - 1))


def spread(values, rows_dev):
    repeat = (lanes_like((rows_dev, LANES), 1) & (rows_dev - 1)) == lanes_like((rows_dev, LANES), 0)
    return jnp.dot(
        values.astype(F32).astype(BF16), repeat.astype(F32).astype(BF16), preferred_element_type=F32
    )


def start_kernel(groups, prior_dev, colidx, live, prior, msg_ref, first_ref, alive_ref, *scratch):
    colidx_ref, live_ref, rows, sems = scratch
    slots, _, rows_dev = colidx_ref.shape
    copies = [
        pltpu.make_async_copy(prior, msg_ref.at[pl.ds(0, prior.shape[0])], sems.at[0]),
        pltpu.make_async_copy(colidx, colidx_ref, sems.at[1]),
        pltpu.make_async_copy(live, live_ref, sems.at[2]),
    ]
    for copy in copies:
        copy.start()
    rows[...] = jnp.zeros(rows.shape, I32)
    copies[1].wait()
    copies[2].wait()
    for j in range(slots):
        rows[j : j + 1] = colidx_ref[j, 0:1]
        rows[8 + j : 9 + j] = lax.shift_right_logical(colidx_ref[j, 1:2], 4)
        rows[16 + j : 17 + j] = colidx_ref[j, 1:2] & 15
        rows[24 + j : 25 + j] = lax.shift_right_logical(colidx_ref[j, 0:1], 4)
        rows[32 + j : 33 + j] = colidx_ref[j, 0:1] & 15
    rows[40:42] = live_ref[...]
    wide = spread(rows[...], rows_dev)
    msg_ref[prior.shape[0] :] = wide[8:24].astype(BF16)
    me, here = lax.axis_index("rows"), lax.axis_index("cols")
    ids = here * slots + lanes_like((8, LANES), 0)
    refs = (wide[24:32] * 16.0 + wide[32:40]).astype(I32)
    live = wide[40:48].astype(I32)
    found = table_at(refs, me, prior_dev, groups // 2)
    first_ref[...] = jnp.where(ids < live[0:1], found, groups * prior_dev)
    alive_ref[...] = (ids < live[1:2]).astype(I32)
    copies[0].wait()


def start(groups, colidx, live, prior):
    rows_dev, slots = colidx.shape[1:]
    prior_dev, probes, order = prior.shape
    table = jax.ShapeDtypeStruct((8, LANES), I32)
    return pl.pallas_call(
        functools.partial(start_kernel, groups, prior_dev),
        out_shape=[jax.ShapeDtypeStruct((prior_dev * probes + TAIL, order), BF16), table, table],
        in_specs=[HBM] * 3,
        out_specs=[VMEM] * 3,
        scratch_shapes=[
            pltpu.VMEM((slots, 2, rows_dev), I32),
            pltpu.VMEM((2, rows_dev), I32),
            pltpu.VMEM((48, rows_dev), I32),
            pltpu.SemaphoreType.DMA((3,)),
        ],
        compiler_params=PARAMS,
        name="start",
    )(*(in_hbm(x) for x in (jnp.transpose(colidx, (2, 0, 1)), live, prior.reshape(-1, order))))


def ranks(mask, within, slots):
    ones = mask.astype(F32).astype(BF16)
    before = jnp.dot(ones, within[0], preferred_element_type=F32)
    count = jnp.dot(ones, within[1], preferred_element_type=F32)
    above = jnp.zeros((1, LANES), F32)
    rows = lanes_like((8, LANES), 0)
    for j in range(slots):
        before = jnp.where(rows == j, before + above, before)
        above = above + count[j : j + 1]
    return before


def route_kernel(groups, cap, slots, prior_dev, owner_ref, alive_ref, *refs):
    tails, outs = refs[:groups], refs[groups : groups + 2]
    want_ref, second_ref, sems = refs[groups + 2 :]
    rows_front = owner_ref.shape[1]
    rows_dev = rows_front // groups
    half = groups // 2
    prior_count = groups * prior_dev
    me = lax.axis_index("rows")
    per = LANES // rows_dev
    lane = lanes_like((8, LANES), 1)
    group_of = lax.shift_right_logical(lane, log2(rows_dev))
    a, b = lanes_like((LANES, LANES), 0), lanes_like((LANES, LANES), 1)
    together = lax.shift_right_logical(a, log2(rows_dev)) == lax.shift_right_logical(b, log2(rows_dev))
    alike = (a & (rows_dev - 1)) == (b & (rows_dev - 1))
    as_bf16 = lambda x: x.astype(F32).astype(BF16)
    within = (as_bf16(together & (a < b)), as_bf16(together))

    def referred(g):
        tail = tails[g][tails[g].shape[0] - TAIL :].astype(F32)
        return (tail[:8] * 16.0 + tail[8:]).astype(I32)

    want_ref[...] = jnp.zeros(want_ref.shape, I32)
    for block in range(groups // per):
        named = referred(block * per)
        for g in range(1, per):
            named = jnp.where(group_of == g, referred(block * per + g), named)
        spot = jnp.full((8, LANES), -1, I32)
        for t in range(rows_dev):
            spot = jnp.where(named == prior_count + owner_ref[0, me * rows_dev + t], t, spot)
        mine = spot >= 0
        rank = ranks(mine, within, slots).astype(I32)
        for q in range(cap):
            held = jnp.where(mine & (rank == q), spot, 0).astype(F32).astype(BF16)
            total = jnp.dot(held, within[1], preferred_element_type=F32)
            want_ref[q : q + 1, block * LANES : (block + 1) * LANES] = jnp.sum(
                total, axis=0, keepdims=True
            ).astype(I32)

    own = referred(0)
    recent = own >= prior_count
    spot = jnp.zeros((8, LANES), I32)
    for t in range(rows_front):
        spot = jnp.where(own == prior_count + owner_ref[0, t], t, spot)
    holder = lax.shift_right_logical(spot, log2(rows_dev)) ^ me
    group = (holder & 1) * half + lax.shift_right_logical(holder, 1)
    rank = jnp.zeros((8, LANES), F32)
    for block in range(groups // per):
        mask = recent & (group == group_of + block * per)
        found = jnp.where(mask, ranks(mask, within, slots), 0.0)
        rank = rank + jnp.dot(found.astype(BF16), as_bf16(alike), preferred_element_type=F32)
    at = jnp.where(
        recent,
        prior_count + group * cap + rank.astype(I32),
        table_at(own, me, prior_dev, half),
    )
    second_ref[...] = jnp.where(alive_ref[...] > 0, at, prior_count + groups * cap)
    copies = [
        pltpu.make_async_copy(x, out, sems.at[i])
        for i, (x, out) in enumerate(zip((want_ref, second_ref), outs))
    ]
    for copy in copies:
        copy.start()
    for copy in copies:
        copy.wait()


def route(groups, cap, slots, prior_dev, owner_map, alive, pieces):
    shapes = [(-(-cap // 8) * 8, owner_map.shape[1]), (8, LANES)]
    return pl.pallas_call(
        functools.partial(route_kernel, groups, cap, slots, prior_dev),
        out_shape=[pltpu.SMEM(a, I32) for a in shapes],
        in_specs=[SMEM] + [VMEM] * (groups + 1),
        out_specs=[SMEM] * 2,
        scratch_shapes=[pltpu.VMEM(a, I32) for a in shapes] + [pltpu.SemaphoreType.DMA((2,))],
        compiler_params=PARAMS,
        name="route",
    )(owner_map, alive, *pieces)


def load_kernel(cols, first_at, blocks, right_side, inverse, *refs):
    outs, at_ref, raw, raw_inverse, sems = refs[:4], refs[4], refs[5], refs[6], refs[7]
    fronts, rows_dev, slots = blocks.shape[:3]
    part = rows_dev // cols
    first = lax.axis_index("cols") * part
    names = pltpu.make_async_copy(first_at, at_ref, sems.at[fronts * cols + 2])
    names.start()
    copies = []
    for f in range(fronts):
        for s in range(cols):
            rows = pl.ds(s * part, part)
            copies.append(
                pltpu.make_async_copy(
                    blocks.at[f, rows], raw.at[f, rows], sems.at[f * cols + s]
                )
            )
    copies += [
        pltpu.make_async_copy(
            inverse.at[:, pl.ds(first, part)], raw_inverse, sems.at[fronts * cols]
        ),
        pltpu.make_async_copy(
            right_side.at[:, pl.ds(first, part)], outs[2], sems.at[fronts * cols + 1]
        ),
    ]
    for copy in copies:
        copy.start()
    for f in range(fronts):
        for s in range(cols):
            copies[f * cols + s].wait()
            for i in range(s * part, (s + 1) * part):
                for j in range(slots):
                    outs[f][i, j] = raw[f, i, j].T
    copies[-2].wait()
    for f in range(fronts):
        for k in range(part):
            outs[3][f, k] = raw_inverse[f, k].T
    copies[-1].wait()
    names.wait()


def load(cols, first_at, blocks, right_side, inverse):
    part = blocks.shape[1] // cols
    shapes = [blocks.shape[1:]] * 2
    shapes += [a.shape[:1] + (part,) + a.shape[2:] for a in (right_side, inverse)]
    kinds = [BF16, BF16, F32, F32]
    return pl.pallas_call(
        functools.partial(load_kernel, cols),
        out_shape=[pltpu.VMEM(a, b) for a, b in zip(shapes, kinds)]
        + [pltpu.SMEM(first_at.shape, I32)],
        in_specs=[VMEM] + [HBM] * 3,
        out_specs=[VMEM] * 4 + [SMEM],
        scratch_shapes=[
            pltpu.VMEM(blocks.shape, BF16),
            pltpu.VMEM(shapes[3], F32),
            pltpu.SemaphoreType.DMA((2 * cols + 3,)),
        ],
        compiler_params=PARAMS,
        cost_estimate=pl.CostEstimate(
            flops=0, transcendentals=0, bytes_accessed=2 * blocks.size * blocks.dtype.itemsize
        ),
        name="load",
    )(first_at, *(in_hbm(x) for x in (blocks, right_side, inverse)))


def partial_kernel(cols, n_early, probes, places, idx_ref, blk, *refs):
    ins, own_ref, msgs, known = refs[:-cols - 1], refs[-cols - 1], refs[-cols:-1], refs[-1]
    rows_dev, slots, order, _ = blk.shape
    part = rows_dev // cols
    here = lax.axis_index("cols")
    for i, (ref, at) in enumerate(zip(ins, places)):
        for k in range((ref.shape[0] - (TAIL if i < n_early else 0)) // probes):
            known[at + k] = ref[k * probes : (k + 1) * probes]
    known[known.shape[0] - 1] = jnp.zeros(known.shape[1:], known.dtype)
    for s in list(range(1, cols)) + [0]:
        first = (here ^ s) * part
        sums = []
        for k in range(part):
            xs = [known[idx_ref[j, first + k]] for j in range(slots)]
            ws = [blk[first + k, j] for j in range(slots)]
            sums.append(
                lax.dot_general(
                    jnp.concatenate(xs, axis=1),
                    jnp.concatenate(ws, axis=0),
                    (((1,), (0,)), ((), ())),
                    preferred_element_type=F32,
                )
            )
        if s == 0:
            for k in range(part):
                own_ref[k] = sums[k]
        else:
            encode_blocks(sums, msgs[s - 1], probes)


def partial_products(name, cols, probes, idx, blocks, early, recent, places):
    rows_dev, slots, order, _ = blocks.shape
    part = rows_dev // cols
    rows = sum(a.shape[0] - TAIL for a in early) + sum(a.shape[0] for a in recent)
    msg = jax.ShapeDtypeStruct((part * probes + TAIL, order), I16)
    out = pl.pallas_call(
        functools.partial(partial_kernel, cols, len(early), probes, places),
        out_shape=[jax.ShapeDtypeStruct((part, probes, order), F32)] + [msg] * (cols - 1),
        in_specs=[SMEM] + [VMEM] * (len(early) + len(recent) + 1),
        out_specs=[VMEM] * cols,
        scratch_shapes=[pltpu.VMEM((rows // probes + 1, probes, order), BF16)],
        compiler_params=PARAMS,
        name=name,
    )(in_smem(idx), blocks, *early, *recent)
    return out[0], out[1:]


def solve_kernel(front, cols, own_ref, *refs):
    msgs, rhs_ref, inv_ref, out_ref = refs[: cols - 1], refs[cols - 1], refs[cols], refs[cols + 1]
    part, probes, _ = own_ref.shape
    total = [own_ref[k] for k in range(part)]
    for msg in msgs:
        total = [a + b for a, b in zip(total, decode_blocks(msg, part, probes))]
    solved = [
        lax.dot_general(
            rhs_ref[front, k] - total[k],
            inv_ref[front, k],
            (((1,), (0,)), ((), ())),
            precision=lax.Precision.HIGHEST,
            preferred_element_type=F32,
        )
        for k in range(part)
    ]
    encode_blocks(solved, out_ref, probes)


def solve_part(front, cols, own, msgs, rhs, inverse):
    part, probes, order = own.shape
    return pl.pallas_call(
        functools.partial(solve_kernel, front, cols),
        out_shape=jax.ShapeDtypeStruct((part * probes + TAIL, order), I16),
        in_specs=[VMEM] * (cols + 2),
        out_specs=VMEM,
        compiler_params=PARAMS,
        name=f"solve_{front}",
    )(own, *msgs, rhs, inverse)


def pack_kernel(sources, groups, cap, sel_ref, *refs):
    cols = len(sources)
    msgs, sends, rows = refs[:cols], refs[cols:-1], refs[-1]
    rows_dev, probes, _ = rows.shape
    part = rows_dev // cols
    here = lax.axis_index("cols")
    for mask, msg in zip(sources, msgs):
        first = (here ^ mask) * part
        for k, value in enumerate(decode_blocks(msg, part, probes)):
            rows[first + k] = value.astype(BF16)
    for m in range(groups):
        for q in range(cap):
            sends[m][q * probes : (q + 1) * probes] = rows[sel_ref[q, m * rows_dev]]


def pack(sources, groups, cap, sel, msgs, shape):
    rows_dev, probes, order = shape
    return pl.pallas_call(
        functools.partial(pack_kernel, sources, groups, cap),
        out_shape=[jax.ShapeDtypeStruct((cap * probes, order), BF16)] * groups,
        in_specs=[SMEM] + [VMEM] * len(msgs),
        out_specs=[VMEM] * groups,
        scratch_shapes=[pltpu.VMEM((rows_dev, probes, order), BF16)],
        compiler_params=PARAMS,
        name="pack",
    )(in_smem(sel), *msgs)


def unpack_kernel(front, sources, *refs):
    msgs, out_ref, rows, sems = refs[: len(sources)], refs[-3], refs[-2], refs[-1]
    part, probes, _ = rows.shape[1:]
    here = lax.axis_index("cols")
    copies = []
    for s, (mask, msg) in enumerate(zip(sources, msgs)):
        for k, value in enumerate(decode_blocks(msg, part, probes)):
            rows[s, k] = value
        to = out_ref.at[front, pl.ds((here ^ mask) * part, part)]
        copies.append(pltpu.make_async_copy(rows.at[s], to, sems.at[s]))
        copies[-1].start()
    for copy in copies:
        copy.wait()


def unpack(front, sources, msgs, shape, base=None):
    _, rows_dev, probes, order = shape
    cols = len(sources)
    rest = [] if base is None else [base]
    return pl.pallas_call(
        functools.partial(unpack_kernel, front, sources),
        out_shape=jax.ShapeDtypeStruct(shape, F32),
        in_specs=[VMEM] * cols + [HBM] * len(rest),
        out_specs=HBM,
        input_output_aliases={} if base is None else {cols: 0},
        scratch_shapes=[
            pltpu.VMEM((cols, rows_dev // cols, probes, order), F32),
            pltpu.SemaphoreType.DMA((cols,)),
        ],
        compiler_params=PARAMS,
        name=f"unpack_{front}",
    )(*msgs, *rest)


def shards(groups, cols, owner_map, colidx, live, blocks, diag_inverse, right_side, prior):
    _, rows_dev, slots, order, _ = blocks.shape
    probes = right_side.shape[2]
    prior_dev = prior.shape[0]
    half = groups // 2
    cap = -(-((slots + 1) // 2) * rows_dev // groups)
    def over_rows(x, mask):
        return lax.ppermute(x, "rows", [(i, i ^ mask) for i in range(groups)])

    def over_cols(x, mask):
        return lax.ppermute(x, "cols", [(i, i ^ mask) for i in range(cols)])

    col_order = list(range(cols - 1, 0, -2)) + list(range(cols - 2, 0, -2))
    row_order = list(range(2, groups, 2)) + list(range(3, groups, 2)) + [1]

    def scatter(xs):
        return [over_cols(xs[m - 1], m) for m in col_order]

    def gather(x):
        masks = [0] + col_order[::-1]
        return masks, [over_cols(x, m) if m else x for m in masks]

    own, first_at, alive = start(groups, colidx, live, prior)
    peers = [m for m in row_order if m % 2 == 0][::-1]
    chips = [over_rows(own, m) for m in peers]
    blocks0, blocks1, rhs, inverse, first_at = load(
        cols, first_at, blocks, right_side, diag_inverse
    )
    chips, blocks0 = lax.optimization_barrier((chips, blocks0))
    chips = [own] + [chips[peers.index(2 * k)] for k in range(1, half)]
    pieces = chips + [over_rows(x, 1) for x in chips]
    early_at = [g * prior_dev for g in range(groups)]
    want, second_at = route(groups, cap, slots, prior_dev, owner_map, alive, pieces)

    own0, msgs0 = partial_products(
        "partial_0", cols, probes, first_at, blocks0, pieces, [], early_at
    )
    coded0 = solve_part(0, cols, own0, scatter(msgs0), rhs, inverse)
    sources, all0 = gather(coded0)

    place = {m: (m & 1) * half + (m >> 1) for m in range(groups)}
    sends = pack(sources, groups, cap, want, all0, right_side.shape[1:])
    recent = [sends[0]] + [over_rows(sends[place[m]], m) for m in row_order]
    recent_at = [groups * prior_dev + place[m] * cap for m in [0] + row_order]
    solved = unpack(0, sources, all0, right_side.shape)

    own1, msgs1 = partial_products(
        "partial_1", cols, probes, second_at, blocks1, pieces, recent, early_at + recent_at
    )
    coded1 = solve_part(1, cols, own1, scatter(msgs1), rhs, inverse)
    sources, all1 = gather(coded1)
    return unpack(1, sources, all1, right_side.shape, solved)


def solution(mesh):
    placed = (
        P(),
        P(None, "rows", "cols"),
        P(None, "rows"),
        P(None, "rows", "cols", None, None),
        P(None, "rows", None, None),
        P(None, "rows", None, None),
        P("rows", None, None),
    )
    body = functools.partial(shards, mesh.shape["rows"], mesh.shape["cols"])
    return jax.shard_map(
        body, mesh=mesh, in_specs=placed, out_specs=P(None, "rows", None, None), check_vma=False
    )
```

```python
import functools

import jax
import jax.numpy as jnp
from jax import lax
from jax.experimental import pallas as pl
from jax.experimental.pallas import tpu as pltpu
from jax.sharding import PartitionSpec as P

F32, BF16, I32, I16 = jnp.float32, jnp.bfloat16, jnp.int32, jnp.int16
VMEM = pl.BlockSpec(memory_space=pltpu.VMEM)
SMEM = pl.BlockSpec(memory_space=pltpu.SMEM)
HBM = pl.BlockSpec(memory_space=pltpu.HBM)
PARAMS = pltpu.CompilerParams(vmem_limit_bytes=16 * 2**20)
STEPS = 128.0
TAIL = 16
LANES = 128


def encode_blocks(values, msg_ref, probes):
    rows = lax.broadcasted_iota(I32, (TAIL, msg_ref.shape[1]), 0)
    tail = jnp.zeros((TAIL, msg_ref.shape[1]), F32)
    for k, value in enumerate(values):
        peak = jnp.maximum(jnp.max(jnp.abs(value), keepdims=True), 2.0**-100)
        level = jnp.ceil(jnp.log2(peak) * STEPS)
        scaled = jnp.round(value * jnp.exp2(15.0 - level * (1.0 / STEPS)))
        scaled = jnp.clip(scaled, -32767.0, 32767.0)
        msg_ref[k * probes : (k + 1) * probes] = scaled.astype(I32).astype(I16)
        tail = jnp.where(rows == k, level, tail)
    msg_ref[len(values) * probes :] = tail.astype(I32).astype(I16)


def decode_blocks(msg_ref, count, probes):
    tail = msg_ref[count * probes :].astype(I32).astype(F32)
    factor = jnp.exp2(tail * (1.0 / STEPS) - 15.0)
    return [
        msg_ref[k * probes : (k + 1) * probes].astype(I32).astype(F32) * factor[k : k + 1]
        for k in range(count)
    ]


def in_hbm(x):
    return pltpu.with_memory_space_constraint(x, pltpu.HBM)


def in_smem(x):
    return pltpu.with_memory_space_constraint(x, pltpu.SMEM)


def log2(n):
    return n.bit_length() - 1


def lanes_like(shape, dim):
    return lax.broadcasted_iota(I32, shape, dim)


def table_at(refs, me, prior_dev, half):
    owner = lax.shift_right_logical(refs, log2(prior_dev)) ^ me
    group = (owner & 1) * half + lax.shift_right_logical(owner, 1)
    return group * prior_dev + (refs & (prior_dev - 1))


def spread(values, rows_dev):
    repeat = (lanes_like((rows_dev, LANES), 1) & (rows_dev - 1)) == lanes_like((rows_dev, LANES), 0)
    return jnp.dot(
        values.astype(F32).astype(BF16), repeat.astype(F32).astype(BF16), preferred_element_type=F32
    )


def start_kernel(colidx, prior, msg_ref, colidx_ref, rows, sems):
    slots, _, rows_dev = colidx_ref.shape
    copies = [
        pltpu.make_async_copy(colidx, colidx_ref, sems.at[0]),
        pltpu.make_async_copy(prior, msg_ref.at[pl.ds(0, prior.shape[0])], sems.at[1]),
    ]
    for copy in copies:
        copy.start()
    rows[...] = jnp.zeros(rows.shape, I32)
    copies[0].wait()
    for j in range(slots):
        rows[j : j + 1] = lax.shift_right_logical(colidx_ref[j, 1:2], 4)
        rows[8 + j : 9 + j] = colidx_ref[j, 1:2] & 15
    msg_ref[prior.shape[0] :] = spread(rows[...], rows_dev).astype(BF16)
    copies[1].wait()


def start(colidx, prior):
    slots, _, rows_dev = colidx.shape
    prior_dev, probes, order = prior.shape
    return pl.pallas_call(
        start_kernel,
        out_shape=jax.ShapeDtypeStruct((prior_dev * probes + TAIL, order), BF16),
        in_specs=[HBM] * 2,
        out_specs=VMEM,
        scratch_shapes=[
            pltpu.VMEM((slots, 2, rows_dev), I32),
            pltpu.VMEM((TAIL, rows_dev), I32),
            pltpu.SemaphoreType.DMA((2,)),
        ],
        compiler_params=PARAMS,
        name="start",
    )(in_hbm(colidx), in_hbm(prior.reshape(-1, order)))


def ranks(mask, within, slots):
    ones = mask.astype(F32).astype(BF16)
    before = jnp.dot(ones, within[0], preferred_element_type=F32)
    count = jnp.dot(ones, within[1], preferred_element_type=F32)
    above = jnp.zeros((1, LANES), F32)
    rows = lanes_like((8, LANES), 0)
    for j in range(slots):
        before = jnp.where(rows == j, before + above, before)
        above = above + count[j : j + 1]
    return before


def route_kernel(groups, cap, slots, prior_dev, owner_ref, alive_ref, *refs):
    tails, outs = refs[:groups], refs[groups : groups + 2]
    want_ref, second_ref, sems = refs[groups + 2 :]
    rows_front = owner_ref.shape[1]
    rows_dev = rows_front // groups
    half = groups // 2
    prior_count = groups * prior_dev
    me = lax.axis_index("rows")
    per = LANES // rows_dev
    lane = lanes_like((8, LANES), 1)
    group_of = lax.shift_right_logical(lane, log2(rows_dev))
    a, b = lanes_like((LANES, LANES), 0), lanes_like((LANES, LANES), 1)
    together = lax.shift_right_logical(a, log2(rows_dev)) == lax.shift_right_logical(b, log2(rows_dev))
    alike = (a & (rows_dev - 1)) == (b & (rows_dev - 1))
    as_bf16 = lambda x: x.astype(F32).astype(BF16)
    within = (as_bf16(together & (a < b)), as_bf16(together))

    def referred(g):
        tail = tails[g][tails[g].shape[0] - TAIL :].astype(F32)
        return (tail[:8] * 16.0 + tail[8:]).astype(I32)

    want_ref[...] = jnp.zeros(want_ref.shape, I32)
    for block in range(groups // per):
        named = referred(block * per)
        for g in range(1, per):
            named = jnp.where(group_of == g, referred(block * per + g), named)
        spot = jnp.full((8, LANES), -1, I32)
        for t in range(rows_dev):
            spot = jnp.where(named == prior_count + owner_ref[0, me * rows_dev + t], t, spot)
        mine = spot >= 0
        rank = ranks(mine, within, slots).astype(I32)
        for q in range(cap):
            held = jnp.where(mine & (rank == q), spot, 0).astype(F32).astype(BF16)
            total = jnp.dot(held, within[1], preferred_element_type=F32)
            want_ref[q : q + 1, block * LANES : (block + 1) * LANES] = jnp.sum(
                total, axis=0, keepdims=True
            ).astype(I32)

    own = referred(0)
    recent = own >= prior_count
    spot = jnp.zeros((8, LANES), I32)
    for t in range(rows_front):
        spot = jnp.where(own == prior_count + owner_ref[0, t], t, spot)
    holder = lax.shift_right_logical(spot, log2(rows_dev)) ^ me
    group = (holder & 1) * half + lax.shift_right_logical(holder, 1)
    rank = jnp.zeros((8, LANES), F32)
    for block in range(groups // per):
        mask = recent & (group == group_of + block * per)
        found = jnp.where(mask, ranks(mask, within, slots), 0.0)
        rank = rank + jnp.dot(found.astype(BF16), as_bf16(alike), preferred_element_type=F32)
    at = jnp.where(
        recent,
        prior_count + group * cap + rank.astype(I32),
        table_at(own, me, prior_dev, half),
    )
    even = ((lax.axis_index("cols") * slots + lanes_like((8, LANES), 0)) & 1) == 0
    dead = jnp.where(even, prior_count + groups * cap, prior_count)
    second_ref[...] = jnp.where(alive_ref[...] > 0, at, dead)
    copies = [
        pltpu.make_async_copy(x, out, sems.at[i])
        for i, (x, out) in enumerate(zip((want_ref, second_ref), outs))
    ]
    for copy in copies:
        copy.start()
    for copy in copies:
        copy.wait()


def route(groups, cap, slots, prior_dev, owner_map, alive, pieces):
    shapes = [(-(-cap // 8) * 8, owner_map.shape[1]), (8, LANES)]
    return pl.pallas_call(
        functools.partial(route_kernel, groups, cap, slots, prior_dev),
        out_shape=[pltpu.SMEM(a, I32) for a in shapes],
        in_specs=[SMEM] + [VMEM] * (groups + 1),
        out_specs=[SMEM] * 2,
        scratch_shapes=[pltpu.VMEM(a, I32) for a in shapes] + [pltpu.SemaphoreType.DMA((2,))],
        compiler_params=PARAMS,
        name="route",
    )(owner_map, alive, *pieces)


def load_kernel(groups, cols, prior_dev, colidx, live, blocks, right_side, inverse, *refs):
    outs, alive_ref, at_ref = refs[:4], refs[4], refs[5]
    colidx_ref, live_ref, rows, first_ref, raw, raw_inverse, sems = refs[6:]
    fronts, rows_dev, slots = blocks.shape[:3]
    part = rows_dev // cols
    mine = pl.ds(lax.axis_index("cols") * part, part)
    count = fronts * cols
    copies = [
        pltpu.make_async_copy(colidx, colidx_ref, sems.at[count]),
        pltpu.make_async_copy(live, live_ref, sems.at[count + 1]),
    ]
    for f in range(fronts):
        for s in range(cols):
            part_rows = pl.ds(s * part, part)
            copies.append(
                pltpu.make_async_copy(
                    blocks.at[f, part_rows], raw.at[f, part_rows], sems.at[f * cols + s]
                )
            )
    copies += [
        pltpu.make_async_copy(inverse.at[:, mine], raw_inverse, sems.at[count + 2]),
        pltpu.make_async_copy(right_side.at[:, mine], outs[2], sems.at[count + 3]),
    ]
    for copy in copies:
        copy.start()
    rows[...] = jnp.zeros(rows.shape, I32)
    copies[0].wait()
    copies[1].wait()
    for j in range(slots):
        rows[j : j + 1] = lax.shift_right_logical(colidx_ref[j, 0:1], 4)
        rows[8 + j : 9 + j] = colidx_ref[j, 0:1] & 15
    rows[16:18] = live_ref[...]
    wide = spread(rows[...], rows_dev)
    ids = lax.axis_index("cols") * slots + lanes_like((8, LANES), 0)
    refs0 = (wide[:8] * 16.0 + wide[8:16]).astype(I32)
    lives = wide[16:24].astype(I32)
    found = table_at(refs0, lax.axis_index("rows"), prior_dev, groups // 2)
    first_ref[...] = jnp.where(ids < lives[0:1], found, groups * prior_dev)
    alive_ref[...] = (ids < lives[1:2]).astype(I32)
    names = pltpu.make_async_copy(first_ref, at_ref, sems.at[count + 4])
    names.start()
    for f in range(fronts):
        for s in range(cols):
            copies[2 + f * cols + s].wait()
            for i in range(s * part, (s + 1) * part):
                for j in range(slots):
                    outs[f][i, j] = raw[f, i, j].T
    copies[-2].wait()
    for f in range(fronts):
        for k in range(part):
            outs[3][f, k] = raw_inverse[f, k].T
    copies[-1].wait()
    names.wait()


def load(groups, cols, prior_dev, colidx, live, blocks, right_side, inverse):
    _, rows_dev, slots = blocks.shape[:3]
    part = rows_dev // cols
    shapes = [blocks.shape[1:]] * 2
    shapes += [a.shape[:1] + (part,) + a.shape[2:] for a in (right_side, inverse)]
    kinds = [BF16, BF16, F32, F32]
    return pl.pallas_call(
        functools.partial(load_kernel, groups, cols, prior_dev),
        out_shape=[pltpu.VMEM(a, b) for a, b in zip(shapes, kinds)]
        + [jax.ShapeDtypeStruct((8, LANES), I32), pltpu.SMEM((8, LANES), I32)],
        in_specs=[HBM] * 5,
        out_specs=[VMEM] * 5 + [SMEM],
        scratch_shapes=[
            pltpu.VMEM((slots, 2, rows_dev), I32),
            pltpu.VMEM((2, rows_dev), I32),
            pltpu.VMEM((24, rows_dev), I32),
            pltpu.VMEM((8, LANES), I32),
            pltpu.VMEM(blocks.shape, BF16),
            pltpu.VMEM(shapes[3], F32),
            pltpu.SemaphoreType.DMA((2 * cols + 5,)),
        ],
        compiler_params=PARAMS,
        cost_estimate=pl.CostEstimate(
            flops=0, transcendentals=0, bytes_accessed=2 * blocks.size * blocks.dtype.itemsize
        ),
        name="load",
    )(*(in_hbm(x) for x in (colidx, live, blocks, right_side, inverse)))


def fill(known, refs, places, tail):
    probes = known.shape[1]
    for ref, at in zip(refs, places):
        for k in range((ref.shape[0] - tail) // probes):
            known[at + k] = ref[k * probes : (k + 1) * probes]
    known[known.shape[0] - 1] = jnp.zeros(known.shape[1:], known.dtype)


def slots_of(parity, slots, here):
    if slots % 2 == 0:
        return slots // 2, lambda q: (2 * q + parity, None)
    shift = (here * slots + parity) & 1
    return (slots + 1) // 2, lambda q: (
        jnp.minimum(2 * q + shift, slots - 1),
        2 * q + shift < slots,
    )


def row_product(known, idx_ref, blk, row, picks, base):
    xs, ws = [], []
    for j, there in picks:
        at = idx_ref[j, row] - base
        if there is not None:
            at = jnp.where(there, at, known.shape[0] - 1)
        xs.append(known[at])
        ws.append(blk[row, j])
    return jnp.dot(
        jnp.concatenate(xs, axis=1), jnp.concatenate(ws, axis=0), preferred_element_type=F32
    )


def partial_kernel(cols, tail, places, base, parity, idx_ref, blk, *refs):
    refs, own_ref, msgs, known = refs[: -cols - 1], refs[-cols - 1], refs[-cols:-1], refs[-1]
    ins, start_from = refs[: len(places)], refs[len(places) :]
    rows_dev, slots = blk.shape[:2]
    part = rows_dev // cols
    here = lax.axis_index("cols")
    fill(known, ins, places, tail)
    if parity is None:
        picks = [(j, None) for j in range(slots)]
    else:
        count, pick = slots_of(parity, slots, here)
        picks = [pick(q) for q in range(count)]
    for s in list(range(1, cols)) + [0]:
        first = (here ^ s) * part
        sums = [row_product(known, idx_ref, blk, first + k, picks, base) for k in range(part)]
        for ref in start_from:
            sums = [x + ref[first + k] for k, x in enumerate(sums)]
        if s == 0:
            for k in range(part):
                own_ref[k] = sums[k]
        else:
            encode_blocks(sums, msgs[s - 1], own_ref.shape[1])


def partial_products(name, cols, probes, idx, blocks, ins, tail, places, base=0, parity=None, start_from=()):
    rows_dev, slots, order, _ = blocks.shape
    part = rows_dev // cols
    rows = sum(a.shape[0] - tail for a in ins) // probes
    msg = jax.ShapeDtypeStruct((part * probes + TAIL, order), I16)
    out = pl.pallas_call(
        functools.partial(partial_kernel, cols, tail, places, base, parity),
        out_shape=[jax.ShapeDtypeStruct((part, probes, order), F32)] + [msg] * (cols - 1),
        in_specs=[SMEM] + [VMEM] * (len(ins) + len(start_from) + 1),
        out_specs=[VMEM] * cols,
        scratch_shapes=[pltpu.VMEM((rows + 1, probes, order), BF16)],
        compiler_params=PARAMS,
        name=name,
    )(in_smem(idx), blocks, *ins, *start_from)
    return out[0], out[1:]


def early_kernel(places, idx_ref, blk, *refs):
    ins, out_ref, known = refs[:-2], refs[-2], refs[-1]
    rows_dev, slots = blk.shape[:2]
    fill(known, ins, places, TAIL)
    count, pick = slots_of(1, slots, lax.axis_index("cols"))
    for i in range(rows_dev):
        out_ref[i] = row_product(known, idx_ref, blk, i, [pick(q) for q in range(count)], 0)


def early_products(probes, idx, blocks, ins, places):
    rows_dev, slots, order, _ = blocks.shape
    rows = sum(a.shape[0] - TAIL for a in ins) // probes
    return pl.pallas_call(
        functools.partial(early_kernel, places),
        out_shape=jax.ShapeDtypeStruct((rows_dev, probes, order), F32),
        in_specs=[SMEM] + [VMEM] * (len(ins) + 1),
        out_specs=VMEM,
        scratch_shapes=[pltpu.VMEM((rows + 1, probes, order), BF16)],
        compiler_params=PARAMS,
        name="early_products",
    )(in_smem(idx), blocks, *ins)


def solve_kernel(front, cols, own_ref, *refs):
    msgs, rhs_ref, inv_ref, out_ref = refs[: cols - 1], refs[cols - 1], refs[cols], refs[cols + 1]
    part, probes, _ = own_ref.shape
    total = [own_ref[k] for k in range(part)]
    for msg in msgs:
        total = [a + b for a, b in zip(total, decode_blocks(msg, part, probes))]
    solved = [
        lax.dot_general(
            rhs_ref[front, k] - total[k],
            inv_ref[front, k],
            (((1,), (0,)), ((), ())),
            precision=lax.Precision.HIGHEST,
            preferred_element_type=F32,
        )
        for k in range(part)
    ]
    encode_blocks(solved, out_ref, probes)


def solve_part(front, cols, own, msgs, rhs, inverse):
    part, probes, order = own.shape
    return pl.pallas_call(
        functools.partial(solve_kernel, front, cols),
        out_shape=jax.ShapeDtypeStruct((part * probes + TAIL, order), I16),
        in_specs=[VMEM] * (cols + 2),
        out_specs=VMEM,
        compiler_params=PARAMS,
        name=f"solve_{front}",
    )(own, *msgs, rhs, inverse)


def pack_kernel(sources, groups, cap, sel_ref, *refs):
    cols = len(sources)
    msgs, sends, rows = refs[:cols], refs[cols:-1], refs[-1]
    rows_dev, probes, _ = rows.shape
    part = rows_dev // cols
    here = lax.axis_index("cols")
    for mask, msg in zip(sources, msgs):
        first = (here ^ mask) * part
        for k, value in enumerate(decode_blocks(msg, part, probes)):
            rows[first + k] = value.astype(BF16)
    for m in range(groups):
        for q in range(cap):
            sends[m][q * probes : (q + 1) * probes] = rows[sel_ref[q, m * rows_dev]]


def pack(sources, groups, cap, sel, msgs, shape):
    rows_dev, probes, order = shape
    return pl.pallas_call(
        functools.partial(pack_kernel, sources, groups, cap),
        out_shape=[jax.ShapeDtypeStruct((cap * probes, order), BF16)] * groups,
        in_specs=[SMEM] + [VMEM] * len(msgs),
        out_specs=[VMEM] * groups,
        scratch_shapes=[pltpu.VMEM((rows_dev, probes, order), BF16)],
        compiler_params=PARAMS,
        name="pack",
    )(in_smem(sel), *msgs)


def unpack_kernel(front, sources, *refs):
    msgs, out_ref, rows, sems = refs[: len(sources)], refs[-3], refs[-2], refs[-1]
    part, probes, _ = rows.shape[1:]
    here = lax.axis_index("cols")
    copies = []
    for s, (mask, msg) in enumerate(zip(sources, msgs)):
        for k, value in enumerate(decode_blocks(msg, part, probes)):
            rows[s, k] = value
        to = out_ref.at[front, pl.ds((here ^ mask) * part, part)]
        copies.append(pltpu.make_async_copy(rows.at[s], to, sems.at[s]))
        copies[-1].start()
    for copy in copies:
        copy.wait()


def unpack(front, sources, msgs, shape, rows_part, base=None):
    _, _, probes, order = shape
    cols, part = len(sources), rows_part
    rest = [] if base is None else [base]
    return pl.pallas_call(
        functools.partial(unpack_kernel, front, sources),
        out_shape=jax.ShapeDtypeStruct(shape, F32),
        in_specs=[VMEM] * cols + [HBM] * len(rest),
        out_specs=HBM,
        input_output_aliases={} if base is None else {cols: 0},
        scratch_shapes=[
            pltpu.VMEM((cols, part, probes, order), F32),
            pltpu.SemaphoreType.DMA((cols,)),
        ],
        compiler_params=PARAMS,
        name=f"unpack_{front}",
    )(*msgs, *rest)


def shards(groups, cols, owner_map, colidx, live, blocks, diag_inverse, right_side, prior):
    _, rows_dev, slots, order, _ = blocks.shape
    probes = right_side.shape[2]
    prior_dev = prior.shape[0]
    half = groups // 2
    cap = -(-((slots + 1) // 2) * rows_dev // groups)
    def over_rows(x, mask):
        return lax.ppermute(x, "rows", [(i, i ^ mask) for i in range(groups)])

    def over_cols(x, mask):
        return lax.ppermute(x, "cols", [(i, i ^ mask) for i in range(cols)])

    col_order = list(range(cols - 1, 0, -2)) + list(range(cols - 2, 0, -2))
    row_order = list(range(2, groups, 2)) + list(range(3, groups, 2)) + [1]

    def scatter(xs):
        return [over_cols(xs[m - 1], m) for m in col_order]

    def gather(x, masks):
        return [over_cols(x, m) if m else x for m in masks]

    colidx = jnp.transpose(colidx, (2, 0, 1))
    own = start(colidx, prior)
    peers = [m for m in row_order if m % 2 == 0][::-1]
    chips = [over_rows(own, m) for m in peers]
    blocks0, blocks1, rhs, inverse, alive, first_at = load(
        groups, cols, prior_dev, colidx, live, blocks, right_side, diag_inverse
    )
    chips, blocks0 = lax.optimization_barrier((chips, blocks0))
    chips = [own] + [chips[peers.index(2 * k)] for k in range(1, half)]
    pieces = chips + [over_rows(x, 1) for x in chips]
    early_at = [g * prior_dev for g in range(groups)]
    want, second_at = route(groups, cap, slots, prior_dev, owner_map, alive, pieces)

    own0, msgs0 = partial_products(
        "partial_0", cols, probes, first_at, blocks0, pieces, TAIL, early_at
    )
    coded0 = solve_part(0, cols, own0, scatter(msgs0), rhs, inverse)
    sources = [0] + col_order[::-1]
    all0 = gather(coded0, sources)

    place = {m: (m & 1) * half + (m >> 1) for m in range(groups)}
    sends = pack(sources, groups, cap, want, all0, right_side.shape[1:])
    recent = [sends[0]] + [over_rows(sends[place[m]], m) for m in row_order]
    recent_at = [place[m] * cap for m in [0] + row_order]
    early = early_products(probes, second_at, blocks1, pieces, early_at)
    part = rows_dev // cols
    solved = unpack(0, sources, all0, right_side.shape, part)

    own1, msgs1 = partial_products(
        "partial_1",
        cols,
        probes,
        second_at,
        blocks1,
        recent,
        0,
        recent_at,
        groups * prior_dev,
        0,
        [early],
    )
    coded1 = solve_part(1, cols, own1, scatter(msgs1), rhs, inverse)
    sources = [0] + col_order[-2::-1] + col_order[-1:]
    all1 = gather(coded1, sources)
    solved = unpack(1, sources[:-1], all1[:-1], right_side.shape, part, solved)
    return unpack(1, sources[-1:], all1[-1:], right_side.shape, part, solved)


def solution(mesh):
    placed = (
        P(),
        P(None, "rows", "cols"),
        P(None, "rows"),
        P(None, "rows", "cols", None, None),
        P(None, "rows", None, None),
        P(None, "rows", None, None),
        P("rows", None, None),
    )
    body = functools.partial(shards, mesh.shape["rows"], mesh.shape["cols"])
    return jax.shard_map(
        body, mesh=mesh, in_specs=placed, out_specs=P(None, "rows", None, None), check_vma=False
    )
```

```python
import functools

import jax
import jax.numpy as jnp
from jax import lax
from jax.experimental import pallas as pl
from jax.experimental.pallas import tpu as pltpu
from jax.sharding import PartitionSpec as P

F32, BF16, I32, I16 = jnp.float32, jnp.bfloat16, jnp.int32, jnp.int16
VMEM = pl.BlockSpec(memory_space=pltpu.VMEM)
SMEM = pl.BlockSpec(memory_space=pltpu.SMEM)
HBM = pl.BlockSpec(memory_space=pltpu.HBM)
PARAMS = pltpu.CompilerParams(vmem_limit_bytes=16 * 2**20)
STEPS = 128.0
TAIL = 16
SCALES = 16
LANES = 128
PIECES = 4


def encode_blocks(values, msg_ref, probes):
    peaks = [jnp.max(jnp.abs(value), axis=0, keepdims=True) for value in values]
    peaks += [jnp.zeros((SCALES - len(peaks), msg_ref.shape[1]), F32)] * (len(peaks) < SCALES)
    peaks = jnp.maximum(jnp.max(jnp.concatenate(peaks), axis=1, keepdims=True), 2.0**-100)
    level = jnp.broadcast_to(jnp.ceil(jnp.log2(peaks) * STEPS), (SCALES, msg_ref.shape[1]))
    factor = jnp.exp2(15.0 - level * (1.0 / STEPS))
    for k, value in enumerate(values):
        scaled = jnp.clip(jnp.round(value * factor[k : k + 1]), -32767.0, 32767.0)
        msg_ref[k * probes : (k + 1) * probes] = scaled.astype(I32).astype(I16)
    msg_ref[len(values) * probes :] = level.astype(I32).astype(I16)


def decode_blocks(msg_ref, count, probes):
    tail = msg_ref[count * probes :].astype(I32).astype(F32)
    factor = jnp.exp2(tail * (1.0 / STEPS) - 15.0)
    return [
        msg_ref[k * probes : (k + 1) * probes].astype(I32).astype(F32) * factor[k : k + 1]
        for k in range(count)
    ]


def in_hbm(x):
    return pltpu.with_memory_space_constraint(x, pltpu.HBM)


def in_smem(x):
    return pltpu.with_memory_space_constraint(x, pltpu.SMEM)


def log2(n):
    return n.bit_length() - 1


def lanes_like(shape, dim):
    return lax.broadcasted_iota(I32, shape, dim)


def table_at(refs, me, prior_dev, half):
    owner = lax.shift_right_logical(refs, log2(prior_dev)) ^ me
    group = (owner & 1) * half + lax.shift_right_logical(owner, 1)
    return group * prior_dev + (refs & (prior_dev - 1))


def spread(values, rows_dev):
    repeat = (lanes_like((rows_dev, LANES), 1) & (rows_dev - 1)) == lanes_like((rows_dev, LANES), 0)
    return jnp.dot(
        values.astype(F32).astype(BF16), repeat.astype(F32).astype(BF16), preferred_element_type=F32
    )


def start_kernel(colidx, prior, msg_ref, colidx_ref, rows, sems):
    slots, _, rows_dev = colidx_ref.shape
    copies = [pltpu.make_async_copy(colidx, colidx_ref, sems.at[0])]
    for i in range(PIECES):
        some = pl.ds(i * (prior.shape[0] // PIECES), prior.shape[0] // PIECES)
        copies.append(pltpu.make_async_copy(prior.at[some], msg_ref.at[some], sems.at[1 + i]))
    for copy in copies:
        copy.start()
    rows[...] = jnp.zeros(rows.shape, I32)
    copies[0].wait()
    for j in range(slots):
        rows[j : j + 1] = lax.shift_right_logical(colidx_ref[j, 1:2], 4)
        rows[8 + j : 9 + j] = colidx_ref[j, 1:2] & 15
    msg_ref[prior.shape[0] :] = spread(rows[...], rows_dev).astype(BF16)
    for copy in copies[1:]:
        copy.wait()


def start(colidx, prior):
    slots, _, rows_dev = colidx.shape
    prior_dev, probes, order = prior.shape
    return pl.pallas_call(
        start_kernel,
        out_shape=jax.ShapeDtypeStruct((prior_dev * probes + TAIL, order), BF16),
        in_specs=[HBM] * 2,
        out_specs=VMEM,
        scratch_shapes=[
            pltpu.VMEM((slots, 2, rows_dev), I32),
            pltpu.VMEM((TAIL, rows_dev), I32),
            pltpu.SemaphoreType.DMA((1 + PIECES,)),
        ],
        compiler_params=PARAMS,
        name="start",
    )(in_hbm(colidx), in_hbm(prior.reshape(-1, order)))


def ranks(mask, within, slots):
    ones = mask.astype(F32).astype(BF16)
    before = jnp.dot(ones, within[0], preferred_element_type=F32)
    count = jnp.dot(ones, within[1], preferred_element_type=F32)
    above = jnp.zeros((1, LANES), F32)
    rows = lanes_like((8, LANES), 0)
    for j in range(slots):
        before = jnp.where(rows == j, before + above, before)
        above = above + count[j : j + 1]
    return before


def route_kernel(groups, cap, slots, prior_dev, owner_ref, alive_ref, *refs):
    tails, outs = refs[:groups], refs[groups : groups + 2]
    want_ref, second_ref, sems = refs[groups + 2 :]
    rows_front = owner_ref.shape[1]
    rows_dev = rows_front // groups
    half = groups // 2
    prior_count = groups * prior_dev
    me = lax.axis_index("rows")
    per = LANES // rows_dev
    lane = lanes_like((8, LANES), 1)
    group_of = lax.shift_right_logical(lane, log2(rows_dev))
    a, b = lanes_like((LANES, LANES), 0), lanes_like((LANES, LANES), 1)
    together = lax.shift_right_logical(a, log2(rows_dev)) == lax.shift_right_logical(b, log2(rows_dev))
    alike = (a & (rows_dev - 1)) == (b & (rows_dev - 1))
    as_bf16 = lambda x: x.astype(F32).astype(BF16)
    within = (as_bf16(together & (a < b)), as_bf16(together))

    def referred(g):
        tail = tails[g][tails[g].shape[0] - TAIL :].astype(F32)
        return (tail[:8] * 16.0 + tail[8:]).astype(I32)

    want_ref[...] = jnp.zeros(want_ref.shape, I32)
    for block in range(groups // per):
        named = referred(block * per)
        for g in range(1, per):
            named = jnp.where(group_of == g, referred(block * per + g), named)
        spot = jnp.full((8, LANES), -1, I32)
        for t in range(rows_dev):
            spot = jnp.where(named == prior_count + owner_ref[0, me * rows_dev + t], t, spot)
        mine = spot >= 0
        rank = ranks(mine, within, slots).astype(I32)
        for q in range(cap):
            held = jnp.where(mine & (rank == q), spot, 0).astype(F32).astype(BF16)
            total = jnp.dot(held, within[1], preferred_element_type=F32)
            want_ref[q : q + 1, block * LANES : (block + 1) * LANES] = jnp.sum(
                total, axis=0, keepdims=True
            ).astype(I32)

    own = referred(0)
    recent = own >= prior_count
    spot = jnp.zeros((8, LANES), I32)
    for t in range(rows_front):
        spot = jnp.where(own == prior_count + owner_ref[0, t], t, spot)
    holder = lax.shift_right_logical(spot, log2(rows_dev)) ^ me
    group = (holder & 1) * half + lax.shift_right_logical(holder, 1)
    rank = jnp.zeros((8, LANES), F32)
    for block in range(groups // per):
        mask = recent & (group == group_of + block * per)
        found = jnp.where(mask, ranks(mask, within, slots), 0.0)
        rank = rank + jnp.dot(found.astype(BF16), as_bf16(alike), preferred_element_type=F32)
    at = jnp.where(
        recent,
        prior_count + group * cap + rank.astype(I32),
        table_at(own, me, prior_dev, half),
    )
    even = ((lax.axis_index("cols") * slots + lanes_like((8, LANES), 0)) & 1) == 0
    dead = jnp.where(even, prior_count + groups * cap, prior_count)
    second_ref[...] = jnp.where(alive_ref[...] > 0, at, dead)
    copies = [
        pltpu.make_async_copy(x, out, sems.at[i])
        for i, (x, out) in enumerate(zip((want_ref, second_ref), outs))
    ]
    for copy in copies:
        copy.start()
    for copy in copies:
        copy.wait()


def route(groups, cap, slots, prior_dev, owner_map, alive, pieces):
    shapes = [(-(-cap // 8) * 8, owner_map.shape[1]), (8, LANES)]
    return pl.pallas_call(
        functools.partial(route_kernel, groups, cap, slots, prior_dev),
        out_shape=[pltpu.SMEM(a, I32) for a in shapes],
        in_specs=[SMEM] + [VMEM] * (groups + 1),
        out_specs=[SMEM] * 2,
        scratch_shapes=[pltpu.VMEM(a, I32) for a in shapes] + [pltpu.SemaphoreType.DMA((2,))],
        compiler_params=PARAMS,
        name="route",
    )(owner_map, alive, *pieces)


def load_kernel(groups, cols, prior_dev, colidx, live, blocks, right_side, inverse, *refs):
    outs, alive_ref, at_ref = refs[:4], refs[4], refs[5]
    colidx_ref, live_ref, rows, first_ref, raw, raw_inverse, sems = refs[6:]
    fronts, rows_dev, slots = blocks.shape[:3]
    part = rows_dev // cols
    mine = pl.ds(lax.axis_index("cols") * part, part)
    count = fronts * cols
    copies = [
        pltpu.make_async_copy(colidx, colidx_ref, sems.at[count]),
        pltpu.make_async_copy(live, live_ref, sems.at[count + 1]),
    ]
    for f in range(fronts):
        for s in range(cols):
            part_rows = pl.ds(s * part, part)
            copies.append(
                pltpu.make_async_copy(
                    blocks.at[f, part_rows], raw.at[f, part_rows], sems.at[f * cols + s]
                )
            )
    copies += [
        pltpu.make_async_copy(inverse.at[:, mine], raw_inverse, sems.at[count + 2]),
        pltpu.make_async_copy(right_side.at[:, mine], outs[2], sems.at[count + 3]),
    ]
    for copy in copies:
        copy.start()
    rows[...] = jnp.zeros(rows.shape, I32)
    copies[0].wait()
    copies[1].wait()
    for j in range(slots):
        rows[j : j + 1] = lax.shift_right_logical(colidx_ref[j, 0:1], 4)
        rows[8 + j : 9 + j] = colidx_ref[j, 0:1] & 15
    rows[16:18] = live_ref[...]
    wide = spread(rows[...], rows_dev)
    ids = lax.axis_index("cols") * slots + lanes_like((8, LANES), 0)
    refs0 = (wide[:8] * 16.0 + wide[8:16]).astype(I32)
    lives = wide[16:24].astype(I32)
    found = table_at(refs0, lax.axis_index("rows"), prior_dev, groups // 2)
    first_ref[...] = jnp.where(ids < lives[0:1], found, groups * prior_dev)
    alive_ref[...] = (ids < lives[1:2]).astype(I32)
    names = pltpu.make_async_copy(first_ref, at_ref, sems.at[count + 4])
    names.start()
    for f in range(fronts):
        for s in range(cols):
            copies[2 + f * cols + s].wait()
            for i in range(s * part, (s + 1) * part):
                for j in range(slots):
                    outs[f][i, j] = raw[f, i, j].T
    copies[-2].wait()
    for f in range(fronts):
        for k in range(part):
            outs[3][f, k] = raw_inverse[f, k].T
    copies[-1].wait()
    names.wait()


def load(groups, cols, prior_dev, colidx, live, blocks, right_side, inverse):
    _, rows_dev, slots = blocks.shape[:3]
    part = rows_dev // cols
    shapes = [blocks.shape[1:]] * 2
    shapes += [a.shape[:1] + (part,) + a.shape[2:] for a in (right_side, inverse)]
    kinds = [BF16, BF16, F32, F32]
    return pl.pallas_call(
        functools.partial(load_kernel, groups, cols, prior_dev),
        out_shape=[pltpu.VMEM(a, b) for a, b in zip(shapes, kinds)]
        + [jax.ShapeDtypeStruct((8, LANES), I32), pltpu.SMEM((8, LANES), I32)],
        in_specs=[HBM] * 5,
        out_specs=[VMEM] * 5 + [SMEM],
        scratch_shapes=[
            pltpu.VMEM((slots, 2, rows_dev), I32),
            pltpu.VMEM((2, rows_dev), I32),
            pltpu.VMEM((24, rows_dev), I32),
            pltpu.VMEM((8, LANES), I32),
            pltpu.VMEM(blocks.shape, BF16),
            pltpu.VMEM(shapes[3], F32),
            pltpu.SemaphoreType.DMA((2 * cols + 5,)),
        ],
        compiler_params=PARAMS,
        cost_estimate=pl.CostEstimate(
            flops=0, transcendentals=0, bytes_accessed=2 * blocks.size * blocks.dtype.itemsize
        ),
        name="load",
    )(*(in_hbm(x) for x in (colidx, live, blocks, right_side, inverse)))


def fill(known, refs, places, tail):
    probes = known.shape[1]
    for ref, at in zip(refs, places):
        for k in range((ref.shape[0] - tail) // probes):
            known[at + k] = ref[k * probes : (k + 1) * probes]
    known[known.shape[0] - 1] = jnp.zeros(known.shape[1:], known.dtype)


def slots_of(parity, slots, here):
    if slots % 2 == 0:
        return slots // 2, lambda q: (2 * q + parity, None)
    shift = (here * slots + parity) & 1
    return (slots + 1) // 2, lambda q: (
        jnp.minimum(2 * q + shift, slots - 1),
        2 * q + shift < slots,
    )


def row_product(known, idx_ref, blk, row, picks, base):
    xs, ws = [], []
    for j, there in picks:
        at = idx_ref[j, row] - base
        if there is not None:
            at = jnp.where(there, at, known.shape[0] - 1)
        xs.append(known[at])
        ws.append(blk[row, j])
    return jnp.dot(
        jnp.concatenate(xs, axis=1), jnp.concatenate(ws, axis=0), preferred_element_type=F32
    )


def partial_kernel(cols, tail, places, base, parity, idx_ref, blk, *refs):
    refs, own_ref, msgs, known = refs[: -cols - 1], refs[-cols - 1], refs[-cols:-1], refs[-1]
    ins, start_from = refs[: len(places)], refs[len(places) :]
    rows_dev, slots = blk.shape[:2]
    part = rows_dev // cols
    here = lax.axis_index("cols")
    fill(known, ins, places, tail)
    if parity is None:
        picks = [(j, None) for j in range(slots)]
    else:
        count, pick = slots_of(parity, slots, here)
        picks = [pick(q) for q in range(count)]
    for s in list(range(1, cols)) + [0]:
        first = (here ^ s) * part
        sums = [row_product(known, idx_ref, blk, first + k, picks, base) for k in range(part)]
        for ref in start_from:
            sums = [x + ref[first + k] for k, x in enumerate(sums)]
        if s == 0:
            for k in range(part):
                own_ref[k] = sums[k]
        else:
            encode_blocks(sums, msgs[s - 1], own_ref.shape[1])


def partial_products(name, cols, probes, idx, blocks, ins, tail, places, base=0, parity=None, start_from=()):
    rows_dev, slots, order, _ = blocks.shape
    part = rows_dev // cols
    rows = sum(a.shape[0] - tail for a in ins) // probes
    msg = jax.ShapeDtypeStruct((part * probes + SCALES, order), I16)
    out = pl.pallas_call(
        functools.partial(partial_kernel, cols, tail, places, base, parity),
        out_shape=[jax.ShapeDtypeStruct((part, probes, order), F32)] + [msg] * (cols - 1),
        in_specs=[SMEM] + [VMEM] * (len(ins) + len(start_from) + 1),
        out_specs=[VMEM] * cols,
        scratch_shapes=[pltpu.VMEM((rows + 1, probes, order), BF16)],
        compiler_params=PARAMS,
        name=name,
    )(in_smem(idx), blocks, *ins, *start_from)
    return out[0], out[1:]


def early_kernel(places, idx_ref, blk, *refs):
    ins, out_ref, known = refs[:-2], refs[-2], refs[-1]
    rows_dev, slots = blk.shape[:2]
    fill(known, ins, places, TAIL)
    count, pick = slots_of(1, slots, lax.axis_index("cols"))
    for i in range(rows_dev):
        out_ref[i] = row_product(known, idx_ref, blk, i, [pick(q) for q in range(count)], 0)


def early_products(probes, idx, blocks, ins, places):
    rows_dev, slots, order, _ = blocks.shape
    rows = sum(a.shape[0] - TAIL for a in ins) // probes
    return pl.pallas_call(
        functools.partial(early_kernel, places),
        out_shape=jax.ShapeDtypeStruct((rows_dev, probes, order), F32),
        in_specs=[SMEM] + [VMEM] * (len(ins) + 1),
        out_specs=VMEM,
        scratch_shapes=[pltpu.VMEM((rows + 1, probes, order), BF16)],
        compiler_params=PARAMS,
        name="early_products",
    )(in_smem(idx), blocks, *ins)


def solve_kernel(front, cols, own_ref, *refs):
    msgs, rhs_ref, inv_ref, out_ref = refs[: cols - 1], refs[cols - 1], refs[cols], refs[cols + 1]
    part, probes, _ = own_ref.shape
    total = [own_ref[k] for k in range(part)]
    for msg in msgs:
        total = [a + b for a, b in zip(total, decode_blocks(msg, part, probes))]
    solved = [
        lax.dot_general(
            rhs_ref[front, k] - total[k],
            inv_ref[front, k],
            (((1,), (0,)), ((), ())),
            precision=lax.Precision.HIGH,
            preferred_element_type=F32,
        )
        for k in range(part)
    ]
    encode_blocks(solved, out_ref, probes)


def solve_part(front, cols, own, msgs, rhs, inverse):
    part, probes, order = own.shape
    return pl.pallas_call(
        functools.partial(solve_kernel, front, cols),
        out_shape=jax.ShapeDtypeStruct((part * probes + SCALES, order), I16),
        in_specs=[VMEM] * (cols + 2),
        out_specs=VMEM,
        compiler_params=PARAMS,
        name=f"solve_{front}",
    )(own, *msgs, rhs, inverse)


def pack_kernel(sources, groups, cap, sel_ref, *refs):
    cols = len(sources)
    msgs, sends, rows = refs[:cols], refs[cols:-1], refs[-1]
    rows_dev, probes, _ = rows.shape
    part = rows_dev // cols
    here = lax.axis_index("cols")
    for mask, msg in zip(sources, msgs):
        first = (here ^ mask) * part
        for k, value in enumerate(decode_blocks(msg, part, probes)):
            rows[first + k] = value.astype(BF16)
    for m in range(groups):
        for q in range(cap):
            sends[m][q * probes : (q + 1) * probes] = rows[sel_ref[q, m * rows_dev]]


def pack(sources, groups, cap, sel, msgs, shape):
    rows_dev, probes, order = shape
    return pl.pallas_call(
        functools.partial(pack_kernel, sources, groups, cap),
        out_shape=[jax.ShapeDtypeStruct((cap * probes, order), BF16)] * groups,
        in_specs=[SMEM] + [VMEM] * len(msgs),
        out_specs=[VMEM] * groups,
        scratch_shapes=[pltpu.VMEM((rows_dev, probes, order), BF16)],
        compiler_params=PARAMS,
        name="pack",
    )(in_smem(sel), *msgs)


def unpack_kernel(front, sources, *refs):
    msgs, out_ref, rows, sems = refs[: len(sources)], refs[-3], refs[-2], refs[-1]
    part, probes, _ = rows.shape[1:]
    here = lax.axis_index("cols")
    copies = []
    for s, (mask, msg) in enumerate(zip(sources, msgs)):
        for k, value in enumerate(decode_blocks(msg, part, probes)):
            rows[s, k] = value
        to = out_ref.at[front, pl.ds((here ^ mask) * part, part)]
        copies.append(pltpu.make_async_copy(rows.at[s], to, sems.at[s]))
        copies[-1].start()
    for copy in copies:
        copy.wait()


def unpack(front, sources, msgs, shape, rows_part, base=None):
    _, _, probes, order = shape
    cols, part = len(sources), rows_part
    rest = [] if base is None else [base]
    return pl.pallas_call(
        functools.partial(unpack_kernel, front, sources),
        out_shape=jax.ShapeDtypeStruct(shape, F32),
        in_specs=[VMEM] * cols + [HBM] * len(rest),
        out_specs=HBM,
        input_output_aliases={} if base is None else {cols: 0},
        scratch_shapes=[
            pltpu.VMEM((cols, part, probes, order), F32),
            pltpu.SemaphoreType.DMA((cols,)),
        ],
        compiler_params=PARAMS,
        name=f"unpack_{front}",
    )(*msgs, *rest)


def shards(groups, cols, owner_map, colidx, live, blocks, diag_inverse, right_side, prior):
    _, rows_dev, slots, order, _ = blocks.shape
    probes = right_side.shape[2]
    prior_dev = prior.shape[0]
    half = groups // 2
    cap = -(-((slots + 1) // 2) * rows_dev // groups)
    def over_rows(x, mask):
        return lax.ppermute(x, "rows", [(i, i ^ mask) for i in range(groups)])

    def over_cols(x, mask):
        return lax.ppermute(x, "cols", [(i, i ^ mask) for i in range(cols)])

    col_order = list(range(cols - 1, 0, -2)) + list(range(cols - 2, 0, -2))
    row_order = list(range(2, groups, 2)) + list(range(3, groups, 2)) + [1]

    def scatter(xs):
        return [over_cols(xs[m - 1], m) for m in col_order]

    def gather(x, masks):
        return [over_cols(x, m) if m else x for m in masks]

    colidx = jnp.transpose(colidx, (2, 0, 1))
    own = start(colidx, prior)
    peers = [m for m in row_order if m % 2 == 0][::-1]
    chips = [over_rows(own, m) for m in peers]
    blocks0, blocks1, rhs, inverse, alive, first_at = load(
        groups, cols, prior_dev, colidx, live, blocks, right_side, diag_inverse
    )
    chips, blocks0 = lax.optimization_barrier((chips, blocks0))
    chips = [own] + [chips[peers.index(2 * k)] for k in range(1, half)]
    pieces = chips + [over_rows(x, 1) for x in chips]
    early_at = [g * prior_dev for g in range(groups)]
    want, second_at = route(groups, cap, slots, prior_dev, owner_map, alive, pieces)

    own0, msgs0 = partial_products(
        "partial_0", cols, probes, first_at, blocks0, pieces, TAIL, early_at
    )
    coded0 = solve_part(0, cols, own0, scatter(msgs0), rhs, inverse)
    sources = [0] + col_order[::-1]
    all0 = gather(coded0, sources)

    place = {m: (m & 1) * half + (m >> 1) for m in range(groups)}
    sends = pack(sources, groups, cap, want, all0, right_side.shape[1:])
    recent = [sends[0]] + [over_rows(sends[place[m]], m) for m in row_order]
    recent_at = [place[m] * cap for m in [0] + row_order]
    early = early_products(probes, second_at, blocks1, pieces, early_at)
    part = rows_dev // cols
    solved = unpack(0, sources, all0, right_side.shape, part)

    own1, msgs1 = partial_products(
        "partial_1",
        cols,
        probes,
        second_at,
        blocks1,
        recent,
        0,
        recent_at,
        groups * prior_dev,
        0,
        [early],
    )
    coded1 = solve_part(1, cols, own1, scatter(msgs1), rhs, inverse)
    sources = [0] + col_order[-2::-1] + col_order[-1:]
    all1 = gather(coded1, sources)
    solved = unpack(1, sources[:-1], all1[:-1], right_side.shape, part, solved)
    return unpack(1, sources[-1:], all1[-1:], right_side.shape, part, solved)


def solution(mesh):
    placed = (
        P(),
        P(None, "rows", "cols"),
        P(None, "rows"),
        P(None, "rows", "cols", None, None),
        P(None, "rows", None, None),
        P(None, "rows", None, None),
        P("rows", None, None),
    )
    body = functools.partial(shards, mesh.shape["rows"], mesh.shape["cols"])
    return jax.shard_map(
        body, mesh=mesh, in_specs=placed, out_specs=P(None, "rows", None, None), check_vma=False
    )
```

```python
import functools

import jax
import jax.numpy as jnp
from jax import lax
from jax.experimental import pallas as pl
from jax.experimental.pallas import tpu as pltpu
from jax.sharding import PartitionSpec as P

F32, BF16, I32, I16 = jnp.float32, jnp.bfloat16, jnp.int32, jnp.int16
VMEM = pl.BlockSpec(memory_space=pltpu.VMEM)
SMEM = pl.BlockSpec(memory_space=pltpu.SMEM)
HBM = pl.BlockSpec(memory_space=pltpu.HBM)
PARAMS = pltpu.CompilerParams(vmem_limit_bytes=16 * 2**20)
STEPS = 128.0
TAIL = 16
SCALES = 16
LANES = 128
PIECES = 4


def peak_of(value):
    return jnp.max(jnp.abs(value), axis=0, keepdims=True)


def scales_of(peaks):
    lanes = peaks[0].shape[1]
    padding = -len(peaks) % SCALES
    peaks = peaks + [jnp.zeros((padding, lanes), F32)] * (padding > 0)
    peaks = jnp.maximum(jnp.max(jnp.concatenate(peaks), axis=1, keepdims=True), 2.0**-100)
    level = jnp.broadcast_to(jnp.ceil(jnp.log2(peaks) * STEPS), (peaks.shape[0], lanes))
    return level, jnp.exp2(15.0 - level * (1.0 / STEPS))


def encode_blocks(values, level, factor, msg_ref, probes):
    for k, value in enumerate(values):
        scaled = jnp.clip(jnp.round(value * factor[k : k + 1]), -32767.0, 32767.0)
        msg_ref[k * probes : (k + 1) * probes] = scaled.astype(I32).astype(I16)
    rows = level.shape[0]
    tail = jnp.concatenate([level, jnp.zeros((SCALES - rows, level.shape[1]), F32)] if rows < SCALES else [level])
    msg_ref[len(values) * probes :] = tail.astype(I32).astype(I16)


def decode_blocks(msg_ref, count, probes):
    tail = msg_ref[count * probes :].astype(I32).astype(F32)
    factor = jnp.exp2(tail * (1.0 / STEPS) - 15.0)
    return [
        msg_ref[k * probes : (k + 1) * probes].astype(I32).astype(F32) * factor[k : k + 1]
        for k in range(count)
    ]


def in_hbm(x):
    return pltpu.with_memory_space_constraint(x, pltpu.HBM)


def in_smem(x):
    return pltpu.with_memory_space_constraint(x, pltpu.SMEM)


def log2(n):
    return n.bit_length() - 1


def lanes_like(shape, dim):
    return lax.broadcasted_iota(I32, shape, dim)


def table_at(refs, me, prior_dev, half):
    owner = lax.shift_right_logical(refs, log2(prior_dev)) ^ me
    group = (owner & 1) * half + lax.shift_right_logical(owner, 1)
    return group * prior_dev + (refs & (prior_dev - 1))


def spread(values, rows_dev):
    repeat = (lanes_like((rows_dev, LANES), 1) & (rows_dev - 1)) == lanes_like((rows_dev, LANES), 0)
    return jnp.dot(
        values.astype(F32).astype(BF16), repeat.astype(F32).astype(BF16), preferred_element_type=F32
    )


def start_kernel(colidx, prior, msg_ref, colidx_ref, rows, sems):
    slots, _, rows_dev = colidx_ref.shape
    copies = [pltpu.make_async_copy(colidx, colidx_ref, sems.at[0])]
    for i in range(PIECES):
        some = pl.ds(i * (prior.shape[0] // PIECES), prior.shape[0] // PIECES)
        copies.append(pltpu.make_async_copy(prior.at[some], msg_ref.at[some], sems.at[1 + i]))
    for copy in copies:
        copy.start()
    rows[...] = jnp.zeros(rows.shape, I32)
    copies[0].wait()
    for j in range(slots):
        rows[j : j + 1] = lax.shift_right_logical(colidx_ref[j, 1:2], 4)
        rows[8 + j : 9 + j] = colidx_ref[j, 1:2] & 15
    msg_ref[prior.shape[0] :] = spread(rows[...], rows_dev).astype(BF16)
    for copy in copies[1:]:
        copy.wait()


def start(colidx, prior):
    slots, _, rows_dev = colidx.shape
    prior_dev, probes, order = prior.shape
    return pl.pallas_call(
        start_kernel,
        out_shape=jax.ShapeDtypeStruct((prior_dev * probes + TAIL, order), BF16),
        in_specs=[HBM] * 2,
        out_specs=VMEM,
        scratch_shapes=[
            pltpu.VMEM((slots, 2, rows_dev), I32),
            pltpu.VMEM((TAIL, rows_dev), I32),
            pltpu.SemaphoreType.DMA((1 + PIECES,)),
        ],
        compiler_params=PARAMS,
        name="start",
    )(in_hbm(colidx), in_hbm(prior.reshape(-1, order)))


def ranks(mask, within, slots):
    ones = mask.astype(F32).astype(BF16)
    before = jnp.dot(ones, within[0], preferred_element_type=F32)
    count = jnp.dot(ones, within[1], preferred_element_type=F32)
    above = jnp.zeros((1, LANES), F32)
    rows = lanes_like((8, LANES), 0)
    for j in range(slots):
        before = jnp.where(rows == j, before + above, before)
        above = above + count[j : j + 1]
    return before


def route_kernel(groups, cap, slots, prior_dev, owner_ref, alive_ref, *refs):
    tails, outs = refs[:groups], refs[groups : groups + 2]
    want_ref, second_ref, sems = refs[groups + 2 :]
    rows_front = owner_ref.shape[1]
    rows_dev = rows_front // groups
    half = groups // 2
    prior_count = groups * prior_dev
    me = lax.axis_index("rows")
    per = LANES // rows_dev
    lane = lanes_like((8, LANES), 1)
    group_of = lax.shift_right_logical(lane, log2(rows_dev))
    a, b = lanes_like((LANES, LANES), 0), lanes_like((LANES, LANES), 1)
    together = lax.shift_right_logical(a, log2(rows_dev)) == lax.shift_right_logical(b, log2(rows_dev))
    alike = (a & (rows_dev - 1)) == (b & (rows_dev - 1))
    as_bf16 = lambda x: x.astype(F32).astype(BF16)
    within = (as_bf16(together & (a < b)), as_bf16(together))

    def referred(g):
        tail = tails[g][tails[g].shape[0] - TAIL :].astype(F32)
        return (tail[:8] * 16.0 + tail[8:]).astype(I32)

    want_ref[...] = jnp.zeros(want_ref.shape, I32)
    for block in range(groups // per):
        named = referred(block * per)
        for g in range(1, per):
            named = jnp.where(group_of == g, referred(block * per + g), named)
        spot = jnp.full((8, LANES), -1, I32)
        for t in range(rows_dev):
            spot = jnp.where(named == prior_count + owner_ref[0, me * rows_dev + t], t, spot)
        mine = spot >= 0
        rank = ranks(mine, within, slots).astype(I32)
        for q in range(cap):
            held = jnp.where(mine & (rank == q), spot, 0).astype(F32).astype(BF16)
            total = jnp.dot(held, within[1], preferred_element_type=F32)
            want_ref[q : q + 1, block * LANES : (block + 1) * LANES] = jnp.sum(
                total, axis=0, keepdims=True
            ).astype(I32)

    own = referred(0)
    recent = own >= prior_count
    spot = jnp.zeros((8, LANES), I32)
    for t in range(rows_front):
        spot = jnp.where(own == prior_count + owner_ref[0, t], t, spot)
    holder = lax.shift_right_logical(spot, log2(rows_dev)) ^ me
    group = (holder & 1) * half + lax.shift_right_logical(holder, 1)
    rank = jnp.zeros((8, LANES), F32)
    for block in range(groups // per):
        mask = recent & (group == group_of + block * per)
        found = jnp.where(mask, ranks(mask, within, slots), 0.0)
        rank = rank + jnp.dot(found.astype(BF16), as_bf16(alike), preferred_element_type=F32)
    at = jnp.where(
        recent,
        prior_count + group * cap + rank.astype(I32),
        table_at(own, me, prior_dev, half),
    )
    even = ((lax.axis_index("cols") * slots + lanes_like((8, LANES), 0)) & 1) == 0
    dead = jnp.where(even, prior_count + groups * cap, prior_count)
    second_ref[...] = jnp.where(alive_ref[...] > 0, at, dead)
    copies = [
        pltpu.make_async_copy(x, out, sems.at[i])
        for i, (x, out) in enumerate(zip((want_ref, second_ref), outs))
    ]
    for copy in copies:
        copy.start()
    for copy in copies:
        copy.wait()


def route(groups, cap, slots, prior_dev, owner_map, alive, pieces):
    shapes = [(-(-cap // 8) * 8, owner_map.shape[1]), (8, LANES)]
    return pl.pallas_call(
        functools.partial(route_kernel, groups, cap, slots, prior_dev),
        out_shape=[pltpu.SMEM(a, I32) for a in shapes],
        in_specs=[SMEM] + [VMEM] * (groups + 1),
        out_specs=[SMEM] * 2,
        scratch_shapes=[pltpu.VMEM(a, I32) for a in shapes] + [pltpu.SemaphoreType.DMA((2,))],
        compiler_params=PARAMS,
        name="route",
    )(owner_map, alive, *pieces)


def load_kernel(groups, cols, prior_dev, colidx, live, blocks, right_side, inverse, *refs):
    outs, alive_ref, at_ref = refs[:4], refs[4], refs[5]
    colidx_ref, live_ref, rows, first_ref, raw, raw_inverse, sems = refs[6:]
    fronts, rows_dev, slots = blocks.shape[:3]
    part = rows_dev // cols
    mine = pl.ds(lax.axis_index("cols") * part, part)
    count = fronts * cols
    copies = [
        pltpu.make_async_copy(colidx, colidx_ref, sems.at[count]),
        pltpu.make_async_copy(live, live_ref, sems.at[count + 1]),
    ]
    for f in range(fronts):
        for s in range(cols):
            part_rows = pl.ds(s * part, part)
            copies.append(
                pltpu.make_async_copy(
                    blocks.at[f, part_rows], raw.at[f, part_rows], sems.at[f * cols + s]
                )
            )
    copies += [
        pltpu.make_async_copy(inverse.at[:, mine], raw_inverse, sems.at[count + 2]),
        pltpu.make_async_copy(right_side.at[:, mine], outs[2], sems.at[count + 3]),
    ]
    for copy in copies:
        copy.start()
    rows[...] = jnp.zeros(rows.shape, I32)
    copies[0].wait()
    copies[1].wait()
    for j in range(slots):
        rows[j : j + 1] = lax.shift_right_logical(colidx_ref[j, 0:1], 4)
        rows[8 + j : 9 + j] = colidx_ref[j, 0:1] & 15
    rows[16:18] = live_ref[...]
    wide = spread(rows[...], rows_dev)
    ids = lax.axis_index("cols") * slots + lanes_like((8, LANES), 0)
    refs0 = (wide[:8] * 16.0 + wide[8:16]).astype(I32)
    lives = wide[16:24].astype(I32)
    found = table_at(refs0, lax.axis_index("rows"), prior_dev, groups // 2)
    first_ref[...] = jnp.where(ids < lives[0:1], found, groups * prior_dev)
    alive_ref[...] = (ids < lives[1:2]).astype(I32)
    names = pltpu.make_async_copy(first_ref, at_ref, sems.at[count + 4])
    names.start()
    for f in range(fronts):
        for s in range(cols):
            copies[2 + f * cols + s].wait()
            for i in range(s * part, (s + 1) * part):
                for j in range(slots):
                    outs[f][i, j] = raw[f, i, j].T
    copies[-2].wait()
    for f in range(fronts):
        for k in range(part):
            outs[3][f, k] = raw_inverse[f, k].T
    copies[-1].wait()
    names.wait()


def load(groups, cols, prior_dev, colidx, live, blocks, right_side, inverse):
    _, rows_dev, slots = blocks.shape[:3]
    part = rows_dev // cols
    shapes = [blocks.shape[1:]] * 2
    shapes += [a.shape[:1] + (part,) + a.shape[2:] for a in (right_side, inverse)]
    kinds = [BF16, BF16, F32, F32]
    return pl.pallas_call(
        functools.partial(load_kernel, groups, cols, prior_dev),
        out_shape=[pltpu.VMEM(a, b) for a, b in zip(shapes, kinds)]
        + [jax.ShapeDtypeStruct((8, LANES), I32), pltpu.SMEM((8, LANES), I32)],
        in_specs=[HBM] * 5,
        out_specs=[VMEM] * 5 + [SMEM],
        scratch_shapes=[
            pltpu.VMEM((slots, 2, rows_dev), I32),
            pltpu.VMEM((2, rows_dev), I32),
            pltpu.VMEM((24, rows_dev), I32),
            pltpu.VMEM((8, LANES), I32),
            pltpu.VMEM(blocks.shape, BF16),
            pltpu.VMEM(shapes[3], F32),
            pltpu.SemaphoreType.DMA((2 * cols + 5,)),
        ],
        compiler_params=PARAMS,
        cost_estimate=pl.CostEstimate(
            flops=0, transcendentals=0, bytes_accessed=2 * blocks.size * blocks.dtype.itemsize
        ),
        name="load",
    )(*(in_hbm(x) for x in (colidx, live, blocks, right_side, inverse)))


def fill(known, refs, places, tail):
    probes = known.shape[1]
    for ref, at in zip(refs, places):
        for k in range((ref.shape[0] - tail) // probes):
            known[at + k] = ref[k * probes : (k + 1) * probes]
    known[known.shape[0] - 1] = jnp.zeros(known.shape[1:], known.dtype)


def slots_of(parity, slots, here):
    if slots % 2 == 0:
        return slots // 2, lambda q: (2 * q + parity, None)
    shift = (here * slots + parity) & 1
    return (slots + 1) // 2, lambda q: (
        jnp.minimum(2 * q + shift, slots - 1),
        2 * q + shift < slots,
    )


def row_product(known, idx_ref, blk, row, picks, base):
    xs, ws = [], []
    for j, there in picks:
        at = idx_ref[j, row] - base
        if there is not None:
            at = jnp.where(there, at, known.shape[0] - 1)
        xs.append(known[at])
        ws.append(blk[row, j])
    return jnp.dot(
        jnp.concatenate(xs, axis=1), jnp.concatenate(ws, axis=0), preferred_element_type=F32
    )


def partial_kernel(cols, tail, places, base, parity, idx_ref, blk, *refs):
    refs, own_ref, msgs, (known, held) = refs[: -cols - 2], refs[-cols - 2], refs[-cols - 1 : -2], refs[-2:]
    ins, start_from = refs[: len(places)], refs[len(places) :]
    rows_dev, slots = blk.shape[:2]
    part = rows_dev // cols
    here = lax.axis_index("cols")
    fill(known, ins, places, tail)
    if parity is None:
        picks = [(j, None) for j in range(slots)]
    else:
        count, pick = slots_of(parity, slots, here)
        picks = [pick(q) for q in range(count)]
    peaks = []
    for s in list(range(1, cols)) + [0]:
        first = (here ^ s) * part
        sums = [row_product(known, idx_ref, blk, first + k, picks, base) for k in range(part)]
        for ref in start_from:
            sums = [x + ref[first + k] for k, x in enumerate(sums)]
        for k in range(part):
            if s == 0:
                own_ref[k] = sums[k]
            else:
                held[(s - 1) * part + k] = sums[k]
                peaks.append(peak_of(sums[k]))
    level, factor = scales_of(peaks)
    for s in range(1, cols):
        at = slice((s - 1) * part, s * part)
        values = [held[k] for k in range(at.start, at.stop)]
        encode_blocks(values, level[at], factor[at], msgs[s - 1], own_ref.shape[1])


def partial_products(name, cols, probes, idx, blocks, ins, tail, places, base=0, parity=None, start_from=()):
    rows_dev, slots, order, _ = blocks.shape
    part = rows_dev // cols
    rows = sum(a.shape[0] - tail for a in ins) // probes
    msg = jax.ShapeDtypeStruct((part * probes + SCALES, order), I16)
    out = pl.pallas_call(
        functools.partial(partial_kernel, cols, tail, places, base, parity),
        out_shape=[jax.ShapeDtypeStruct((part, probes, order), F32)] + [msg] * (cols - 1),
        in_specs=[SMEM] + [VMEM] * (len(ins) + len(start_from) + 1),
        out_specs=[VMEM] * cols,
        scratch_shapes=[
            pltpu.VMEM((rows + 1, probes, order), BF16),
            pltpu.VMEM((rows_dev - part, probes, order), F32),
        ],
        compiler_params=PARAMS,
        name=name,
    )(in_smem(idx), blocks, *ins, *start_from)
    return out[0], out[1:]


def early_kernel(places, idx_ref, blk, *refs):
    ins, out_ref, known = refs[:-2], refs[-2], refs[-1]
    rows_dev, slots = blk.shape[:2]
    fill(known, ins, places, TAIL)
    count, pick = slots_of(1, slots, lax.axis_index("cols"))
    for i in range(rows_dev):
        out_ref[i] = row_product(known, idx_ref, blk, i, [pick(q) for q in range(count)], 0)


def early_products(probes, idx, blocks, ins, places):
    rows_dev, slots, order, _ = blocks.shape
    rows = sum(a.shape[0] - TAIL for a in ins) // probes
    return pl.pallas_call(
        functools.partial(early_kernel, places),
        out_shape=jax.ShapeDtypeStruct((rows_dev, probes, order), F32),
        in_specs=[SMEM] + [VMEM] * (len(ins) + 1),
        out_specs=VMEM,
        scratch_shapes=[pltpu.VMEM((rows + 1, probes, order), BF16)],
        compiler_params=PARAMS,
        name="early_products",
    )(in_smem(idx), blocks, *ins)


def solve_kernel(front, cols, own_ref, *refs):
    msgs, rhs_ref, inv_ref, out_ref = refs[: cols - 1], refs[cols - 1], refs[cols], refs[cols + 1]
    part, probes, _ = own_ref.shape
    total = [own_ref[k] for k in range(part)]
    for msg in msgs:
        total = [a + b for a, b in zip(total, decode_blocks(msg, part, probes))]
    solved = [
        lax.dot_general(
            rhs_ref[front, k] - total[k],
            inv_ref[front, k],
            (((1,), (0,)), ((), ())),
            precision=lax.Precision.HIGH,
            preferred_element_type=F32,
        )
        for k in range(part)
    ]
    level, factor = scales_of([peak_of(value) for value in solved])
    encode_blocks(solved, level, factor, out_ref, probes)


def solve_part(front, cols, own, msgs, rhs, inverse):
    part, probes, order = own.shape
    return pl.pallas_call(
        functools.partial(solve_kernel, front, cols),
        out_shape=jax.ShapeDtypeStruct((part * probes + SCALES, order), I16),
        in_specs=[VMEM] * (cols + 2),
        out_specs=VMEM,
        compiler_params=PARAMS,
        name=f"solve_{front}",
    )(own, *msgs, rhs, inverse)


def pack_kernel(sources, groups, cap, sel_ref, *refs):
    cols = len(sources)
    msgs, sends, rows = refs[:cols], refs[cols:-1], refs[-1]
    rows_dev, probes, _ = rows.shape
    part = rows_dev // cols
    here = lax.axis_index("cols")
    for mask, msg in zip(sources, msgs):
        first = (here ^ mask) * part
        for k, value in enumerate(decode_blocks(msg, part, probes)):
            rows[first + k] = value.astype(BF16)
    for m in range(groups):
        for q in range(cap):
            sends[m][q * probes : (q + 1) * probes] = rows[sel_ref[q, m * rows_dev]]


def pack(sources, groups, cap, sel, msgs, shape):
    rows_dev, probes, order = shape
    return pl.pallas_call(
        functools.partial(pack_kernel, sources, groups, cap),
        out_shape=[jax.ShapeDtypeStruct((cap * probes, order), BF16)] * groups,
        in_specs=[SMEM] + [VMEM] * len(msgs),
        out_specs=[VMEM] * groups,
        scratch_shapes=[pltpu.VMEM((rows_dev, probes, order), BF16)],
        compiler_params=PARAMS,
        name="pack",
    )(in_smem(sel), *msgs)


def unpack_kernel(front, sources, *refs):
    msgs, out_ref, rows, sems = refs[: len(sources)], refs[-3], refs[-2], refs[-1]
    part, probes, _ = rows.shape[1:]
    here = lax.axis_index("cols")
    copies = []
    for s, (mask, msg) in enumerate(zip(sources, msgs)):
        for k, value in enumerate(decode_blocks(msg, part, probes)):
            rows[s, k] = value
        to = out_ref.at[front, pl.ds((here ^ mask) * part, part)]
        copies.append(pltpu.make_async_copy(rows.at[s], to, sems.at[s]))
        copies[-1].start()
    for copy in copies:
        copy.wait()


def unpack(front, sources, msgs, shape, rows_part, base=None):
    _, _, probes, order = shape
    cols, part = len(sources), rows_part
    rest = [] if base is None else [base]
    return pl.pallas_call(
        functools.partial(unpack_kernel, front, sources),
        out_shape=jax.ShapeDtypeStruct(shape, F32),
        in_specs=[VMEM] * cols + [HBM] * len(rest),
        out_specs=HBM,
        input_output_aliases={} if base is None else {cols: 0},
        scratch_shapes=[
            pltpu.VMEM((cols, part, probes, order), F32),
            pltpu.SemaphoreType.DMA((cols,)),
        ],
        compiler_params=PARAMS,
        name=f"unpack_{front}",
    )(*msgs, *rest)


def shards(groups, cols, owner_map, colidx, live, blocks, diag_inverse, right_side, prior):
    _, rows_dev, slots, order, _ = blocks.shape
    probes = right_side.shape[2]
    prior_dev = prior.shape[0]
    half = groups // 2
    cap = -(-((slots + 1) // 2) * rows_dev // groups)
    def over_rows(x, mask):
        return lax.ppermute(x, "rows", [(i, i ^ mask) for i in range(groups)])

    def over_cols(x, mask):
        return lax.ppermute(x, "cols", [(i, i ^ mask) for i in range(cols)])

    col_order = list(range(cols - 1, 0, -2)) + list(range(cols - 2, 0, -2))
    row_order = list(range(2, groups, 2)) + list(range(3, groups, 2)) + [1]

    def scatter(xs):
        return [over_cols(xs[m - 1], m) for m in col_order]

    def gather(x, masks):
        return [over_cols(x, m) if m else x for m in masks]

    colidx = jnp.transpose(colidx, (2, 0, 1))
    own = start(colidx, prior)
    peers = [m for m in row_order if m % 2 == 0][::-1]
    chips = [over_rows(own, m) for m in peers]
    blocks0, blocks1, rhs, inverse, alive, first_at = load(
        groups, cols, prior_dev, colidx, live, blocks, right_side, diag_inverse
    )
    chips, blocks0 = lax.optimization_barrier((chips, blocks0))
    chips = [own] + [chips[peers.index(2 * k)] for k in range(1, half)]
    pieces = chips + [over_rows(x, 1) for x in chips]
    early_at = [g * prior_dev for g in range(groups)]
    want, second_at = route(groups, cap, slots, prior_dev, owner_map, alive, pieces)

    own0, msgs0 = partial_products(
        "partial_0", cols, probes, first_at, blocks0, pieces, TAIL, early_at
    )
    coded0 = solve_part(0, cols, own0, scatter(msgs0), rhs, inverse)
    sources = [0] + col_order[::-1]
    all0 = gather(coded0, sources)

    place = {m: (m & 1) * half + (m >> 1) for m in range(groups)}
    sends = pack(sources, groups, cap, want, all0, right_side.shape[1:])
    recent = [sends[0]] + [over_rows(sends[place[m]], m) for m in row_order]
    recent_at = [place[m] * cap for m in [0] + row_order]
    early = early_products(probes, second_at, blocks1, pieces, early_at)
    part = rows_dev // cols
    solved = unpack(0, sources, all0, right_side.shape, part)

    own1, msgs1 = partial_products(
        "partial_1",
        cols,
        probes,
        second_at,
        blocks1,
        recent,
        0,
        recent_at,
        groups * prior_dev,
        0,
        [early],
    )
    coded1 = solve_part(1, cols, own1, scatter(msgs1), rhs, inverse)
    sources = [0] + col_order[:1] + col_order[:0:-1]
    all1 = gather(coded1, sources)
    solved = unpack(1, sources[:2], all1[:2], right_side.shape, part, solved)
    return unpack(1, sources[2:], all1[2:], right_side.shape, part, solved)


def solution(mesh):
    placed = (
        P(),
        P(None, "rows", "cols"),
        P(None, "rows"),
        P(None, "rows", "cols", None, None),
        P(None, "rows", None, None),
        P(None, "rows", None, None),
        P("rows", None, None),
    )
    body = functools.partial(shards, mesh.shape["rows"], mesh.shape["cols"])
    return jax.shard_map(
        body, mesh=mesh, in_specs=placed, out_specs=P(None, "rows", None, None), check_vma=False
    )
```

```python
import functools

import jax
import jax.numpy as jnp
from jax import lax
from jax.experimental import pallas as pl
from jax.experimental.pallas import tpu as pltpu
from jax.sharding import PartitionSpec as P

F32, BF16, I32, I16 = jnp.float32, jnp.bfloat16, jnp.int32, jnp.int16
VMEM = pl.BlockSpec(memory_space=pltpu.VMEM)
SMEM = pl.BlockSpec(memory_space=pltpu.SMEM)
HBM = pl.BlockSpec(memory_space=pltpu.HBM)
PARAMS = pltpu.CompilerParams(vmem_limit_bytes=16 * 2**20)
STEPS = 128.0
TAIL = 16
SCALES = 16
LANES = 128
PIECES = 4


def encode_blocks(values, msg_ref, probes):
    peaks = [jnp.max(jnp.abs(value), axis=0, keepdims=True) for value in values]
    peaks += [jnp.zeros((SCALES - len(peaks), msg_ref.shape[1]), F32)] * (len(peaks) < SCALES)
    peaks = jnp.maximum(jnp.max(jnp.concatenate(peaks), axis=1, keepdims=True), 2.0**-100)
    level = jnp.broadcast_to(jnp.ceil(jnp.log2(peaks) * STEPS), (SCALES, msg_ref.shape[1]))
    factor = jnp.exp2(15.0 - level * (1.0 / STEPS))
    for k, value in enumerate(values):
        scaled = jnp.clip(jnp.round(value * factor[k : k + 1]), -32767.0, 32767.0)
        msg_ref[k * probes : (k + 1) * probes] = scaled.astype(I32).astype(I16)
    msg_ref[len(values) * probes :] = level.astype(I32).astype(I16)


def decode_blocks(msg_ref, count, probes):
    tail = msg_ref[count * probes :].astype(I32).astype(F32)
    factor = jnp.exp2(tail * (1.0 / STEPS) - 15.0)
    return [
        msg_ref[k * probes : (k + 1) * probes].astype(I32).astype(F32) * factor[k : k + 1]
        for k in range(count)
    ]


def in_hbm(x):
    return pltpu.with_memory_space_constraint(x, pltpu.HBM)


def in_smem(x):
    return pltpu.with_memory_space_constraint(x, pltpu.SMEM)


def log2(n):
    return n.bit_length() - 1


def lanes_like(shape, dim):
    return lax.broadcasted_iota(I32, shape, dim)


def table_at(refs, me, prior_dev, half):
    owner = lax.shift_right_logical(refs, log2(prior_dev)) ^ me
    group = (owner & 1) * half + lax.shift_right_logical(owner, 1)
    return group * prior_dev + (refs & (prior_dev - 1))


def spread(values, rows_dev):
    repeat = (lanes_like((rows_dev, LANES), 1) & (rows_dev - 1)) == lanes_like((rows_dev, LANES), 0)
    return jnp.dot(
        values.astype(F32).astype(BF16), repeat.astype(F32).astype(BF16), preferred_element_type=F32
    )


def start_kernel(colidx, prior, msg_ref, colidx_ref, rows, sems):
    slots, _, rows_dev = colidx_ref.shape
    copies = [pltpu.make_async_copy(colidx, colidx_ref, sems.at[0])]
    for i in range(PIECES):
        some = pl.ds(i * (prior.shape[0] // PIECES), prior.shape[0] // PIECES)
        copies.append(pltpu.make_async_copy(prior.at[some], msg_ref.at[some], sems.at[1 + i]))
    for copy in copies:
        copy.start()
    rows[...] = jnp.zeros(rows.shape, I32)
    copies[0].wait()
    for j in range(slots):
        rows[j : j + 1] = lax.shift_right_logical(colidx_ref[j, 1:2], 4)
        rows[8 + j : 9 + j] = colidx_ref[j, 1:2] & 15
    msg_ref[prior.shape[0] :] = spread(rows[...], rows_dev).astype(BF16)
    for copy in copies[1:]:
        copy.wait()


def start(colidx, prior):
    slots, _, rows_dev = colidx.shape
    prior_dev, probes, order = prior.shape
    return pl.pallas_call(
        start_kernel,
        out_shape=jax.ShapeDtypeStruct((prior_dev * probes + TAIL, order), BF16),
        in_specs=[HBM] * 2,
        out_specs=VMEM,
        scratch_shapes=[
            pltpu.VMEM((slots, 2, rows_dev), I32),
            pltpu.VMEM((TAIL, rows_dev), I32),
            pltpu.SemaphoreType.DMA((1 + PIECES,)),
        ],
        compiler_params=PARAMS,
        name="start",
    )(in_hbm(colidx), in_hbm(prior.reshape(-1, order)))


def ranks(mask, within, slots):
    ones = mask.astype(F32).astype(BF16)
    before = jnp.dot(ones, within[0], preferred_element_type=F32)
    count = jnp.dot(ones, within[1], preferred_element_type=F32)
    above = jnp.zeros((1, LANES), F32)
    rows = lanes_like((8, LANES), 0)
    for j in range(slots):
        before = jnp.where(rows == j, before + above, before)
        above = above + count[j : j + 1]
    return before


def route_kernel(groups, cap, slots, prior_dev, owner_ref, alive_ref, *refs):
    tails, outs = refs[:groups], refs[groups : groups + 2]
    want_ref, second_ref, sems = refs[groups + 2 :]
    rows_front = owner_ref.shape[1]
    rows_dev = rows_front // groups
    half = groups // 2
    prior_count = groups * prior_dev
    me = lax.axis_index("rows")
    per = LANES // rows_dev
    lane = lanes_like((8, LANES), 1)
    group_of = lax.shift_right_logical(lane, log2(rows_dev))
    a, b = lanes_like((LANES, LANES), 0), lanes_like((LANES, LANES), 1)
    together = lax.shift_right_logical(a, log2(rows_dev)) == lax.shift_right_logical(b, log2(rows_dev))
    alike = (a & (rows_dev - 1)) == (b & (rows_dev - 1))
    as_bf16 = lambda x: x.astype(F32).astype(BF16)
    within = (as_bf16(together & (a < b)), as_bf16(together))

    def referred(g):
        tail = tails[g][tails[g].shape[0] - TAIL :].astype(F32)
        return (tail[:8] * 16.0 + tail[8:]).astype(I32)

    want_ref[...] = jnp.zeros(want_ref.shape, I32)
    for block in range(groups // per):
        named = referred(block * per)
        for g in range(1, per):
            named = jnp.where(group_of == g, referred(block * per + g), named)
        spot = jnp.full((8, LANES), -1, I32)
        for t in range(rows_dev):
            spot = jnp.where(named == prior_count + owner_ref[0, me * rows_dev + t], t, spot)
        mine = spot >= 0
        rank = ranks(mine, within, slots).astype(I32)
        for q in range(cap):
            held = jnp.where(mine & (rank == q), spot, 0).astype(F32).astype(BF16)
            total = jnp.dot(held, within[1], preferred_element_type=F32)
            want_ref[q : q + 1, block * LANES : (block + 1) * LANES] = jnp.sum(
                total, axis=0, keepdims=True
            ).astype(I32)

    own = referred(0)
    recent = own >= prior_count
    spot = jnp.zeros((8, LANES), I32)
    for t in range(rows_front):
        spot = jnp.where(own == prior_count + owner_ref[0, t], t, spot)
    holder = lax.shift_right_logical(spot, log2(rows_dev)) ^ me
    group = (holder & 1) * half + lax.shift_right_logical(holder, 1)
    rank = jnp.zeros((8, LANES), F32)
    for block in range(groups // per):
        mask = recent & (group == group_of + block * per)
        found = jnp.where(mask, ranks(mask, within, slots), 0.0)
        rank = rank + jnp.dot(found.astype(BF16), as_bf16(alike), preferred_element_type=F32)
    at = jnp.where(
        recent,
        prior_count + group * cap + rank.astype(I32),
        table_at(own, me, prior_dev, half),
    )
    even = ((lax.axis_index("cols") * slots + lanes_like((8, LANES), 0)) & 1) == 0
    dead = jnp.where(even, prior_count + groups * cap, prior_count)
    second_ref[...] = jnp.where(alive_ref[...] > 0, at, dead)
    copies = [
        pltpu.make_async_copy(x, out, sems.at[i])
        for i, (x, out) in enumerate(zip((want_ref, second_ref), outs))
    ]
    for copy in copies:
        copy.start()
    for copy in copies:
        copy.wait()


def route(groups, cap, slots, prior_dev, owner_map, alive, pieces):
    shapes = [(-(-cap // 8) * 8, owner_map.shape[1]), (8, LANES)]
    return pl.pallas_call(
        functools.partial(route_kernel, groups, cap, slots, prior_dev),
        out_shape=[pltpu.SMEM(a, I32) for a in shapes],
        in_specs=[SMEM] + [VMEM] * (groups + 1),
        out_specs=[SMEM] * 2,
        scratch_shapes=[pltpu.VMEM(a, I32) for a in shapes] + [pltpu.SemaphoreType.DMA((2,))],
        compiler_params=PARAMS,
        name="route",
    )(owner_map, alive, *pieces)


def load_kernel(groups, cols, prior_dev, colidx, live, blocks, right_side, inverse, *refs):
    outs, alive_ref, at_ref = refs[:4], refs[4], refs[5]
    colidx_ref, live_ref, rows, first_ref, raw, raw_inverse, sems = refs[6:]
    fronts, rows_dev, slots = blocks.shape[:3]
    part = rows_dev // cols
    mine = pl.ds(lax.axis_index("cols") * part, part)
    count = fronts * cols
    copies = [
        pltpu.make_async_copy(colidx, colidx_ref, sems.at[count]),
        pltpu.make_async_copy(live, live_ref, sems.at[count + 1]),
    ]
    for f in range(fronts):
        for s in range(cols):
            part_rows = pl.ds(s * part, part)
            copies.append(
                pltpu.make_async_copy(
                    blocks.at[f, part_rows], raw.at[f, part_rows], sems.at[f * cols + s]
                )
            )
    copies += [
        pltpu.make_async_copy(inverse.at[:, mine], raw_inverse, sems.at[count + 2]),
        pltpu.make_async_copy(right_side.at[:, mine], outs[2], sems.at[count + 3]),
    ]
    for copy in copies:
        copy.start()
    rows[...] = jnp.zeros(rows.shape, I32)
    copies[0].wait()
    copies[1].wait()
    for j in range(slots):
        rows[j : j + 1] = lax.shift_right_logical(colidx_ref[j, 0:1], 4)
        rows[8 + j : 9 + j] = colidx_ref[j, 0:1] & 15
    rows[16:18] = live_ref[...]
    wide = spread(rows[...], rows_dev)
    ids = lax.axis_index("cols") * slots + lanes_like((8, LANES), 0)
    refs0 = (wide[:8] * 16.0 + wide[8:16]).astype(I32)
    lives = wide[16:24].astype(I32)
    found = table_at(refs0, lax.axis_index("rows"), prior_dev, groups // 2)
    first_ref[...] = jnp.where(ids < lives[0:1], found, groups * prior_dev)
    alive_ref[...] = (ids < lives[1:2]).astype(I32)
    names = pltpu.make_async_copy(first_ref, at_ref, sems.at[count + 4])
    names.start()
    for f in range(fronts):
        for s in range(cols):
            copies[2 + f * cols + s].wait()
            for i in range(s * part, (s + 1) * part):
                for j in range(slots):
                    outs[f][i, j] = raw[f, i, j].T
    copies[-2].wait()
    for f in range(fronts):
        for k in range(part):
            outs[3][f, k] = raw_inverse[f, k].T
    copies[-1].wait()
    names.wait()


def load(groups, cols, prior_dev, colidx, live, blocks, right_side, inverse):
    _, rows_dev, slots = blocks.shape[:3]
    part = rows_dev // cols
    shapes = [blocks.shape[1:]] * 2
    shapes += [a.shape[:1] + (part,) + a.shape[2:] for a in (right_side, inverse)]
    kinds = [BF16, BF16, F32, F32]
    return pl.pallas_call(
        functools.partial(load_kernel, groups, cols, prior_dev),
        out_shape=[pltpu.VMEM(a, b) for a, b in zip(shapes, kinds)]
        + [jax.ShapeDtypeStruct((8, LANES), I32), pltpu.SMEM((8, LANES), I32)],
        in_specs=[HBM] * 5,
        out_specs=[VMEM] * 5 + [SMEM],
        scratch_shapes=[
            pltpu.VMEM((slots, 2, rows_dev), I32),
            pltpu.VMEM((2, rows_dev), I32),
            pltpu.VMEM((24, rows_dev), I32),
            pltpu.VMEM((8, LANES), I32),
            pltpu.VMEM(blocks.shape, BF16),
            pltpu.VMEM(shapes[3], F32),
            pltpu.SemaphoreType.DMA((2 * cols + 5,)),
        ],
        compiler_params=PARAMS,
        cost_estimate=pl.CostEstimate(
            flops=0, transcendentals=0, bytes_accessed=2 * blocks.size * blocks.dtype.itemsize
        ),
        name="load",
    )(*(in_hbm(x) for x in (colidx, live, blocks, right_side, inverse)))


def fill(known, refs, places, tail):
    probes = known.shape[1]
    for ref, at in zip(refs, places):
        for k in range((ref.shape[0] - tail) // probes):
            known[at + k] = ref[k * probes : (k + 1) * probes]
    known[known.shape[0] - 1] = jnp.zeros(known.shape[1:], known.dtype)


def slots_of(parity, slots, here):
    if slots % 2 == 0:
        return slots // 2, lambda q: (2 * q + parity, None)
    shift = (here * slots + parity) & 1
    return (slots + 1) // 2, lambda q: (
        jnp.minimum(2 * q + shift, slots - 1),
        2 * q + shift < slots,
    )


def row_product(known, idx_ref, blk, row, picks, base):
    xs, ws = [], []
    for j, there in picks:
        at = idx_ref[j, row] - base
        if there is not None:
            at = jnp.where(there, at, known.shape[0] - 1)
        xs.append(known[at])
        ws.append(blk[row, j])
    return jnp.dot(
        jnp.concatenate(xs, axis=1), jnp.concatenate(ws, axis=0), preferred_element_type=F32
    )


def partial_kernel(cols, tail, places, base, parity, idx_ref, blk, *refs):
    refs, own_ref, msgs, known = refs[: -cols - 1], refs[-cols - 1], refs[-cols:-1], refs[-1]
    ins, start_from = refs[: len(places)], refs[len(places) :]
    rows_dev, slots = blk.shape[:2]
    part = rows_dev // cols
    here = lax.axis_index("cols")
    fill(known, ins, places, tail)
    if parity is None:
        picks = [(j, None) for j in range(slots)]
    else:
        count, pick = slots_of(parity, slots, here)
        picks = [pick(q) for q in range(count)]
    for s in list(range(1, cols)) + [0]:
        first = (here ^ s) * part
        sums = [row_product(known, idx_ref, blk, first + k, picks, base) for k in range(part)]
        for ref in start_from:
            sums = [x + ref[first + k] for k, x in enumerate(sums)]
        if s == 0:
            for k in range(part):
                own_ref[k] = sums[k]
        else:
            encode_blocks(sums, msgs[s - 1], own_ref.shape[1])


def partial_products(name, cols, probes, idx, blocks, ins, tail, places, base=0, parity=None, start_from=()):
    rows_dev, slots, order, _ = blocks.shape
    part = rows_dev // cols
    rows = sum(a.shape[0] - tail for a in ins) // probes
    msg = jax.ShapeDtypeStruct((part * probes + SCALES, order), I16)
    out = pl.pallas_call(
        functools.partial(partial_kernel, cols, tail, places, base, parity),
        out_shape=[jax.ShapeDtypeStruct((part, probes, order), F32)] + [msg] * (cols - 1),
        in_specs=[SMEM] + [VMEM] * (len(ins) + len(start_from) + 1),
        out_specs=[VMEM] * cols,
        scratch_shapes=[pltpu.VMEM((rows + 1, probes, order), BF16)],
        compiler_params=PARAMS,
        name=name,
    )(in_smem(idx), blocks, *ins, *start_from)
    return out[0], out[1:]


def early_kernel(places, idx_ref, blk, *refs):
    ins, out_ref, known = refs[:-2], refs[-2], refs[-1]
    rows_dev, slots = blk.shape[:2]
    fill(known, ins, places, TAIL)
    count, pick = slots_of(1, slots, lax.axis_index("cols"))
    for i in range(rows_dev):
        out_ref[i] = row_product(known, idx_ref, blk, i, [pick(q) for q in range(count)], 0)


def early_products(probes, idx, blocks, ins, places):
    rows_dev, slots, order, _ = blocks.shape
    rows = sum(a.shape[0] - TAIL for a in ins) // probes
    return pl.pallas_call(
        functools.partial(early_kernel, places),
        out_shape=jax.ShapeDtypeStruct((rows_dev, probes, order), F32),
        in_specs=[SMEM] + [VMEM] * (len(ins) + 1),
        out_specs=VMEM,
        scratch_shapes=[pltpu.VMEM((rows + 1, probes, order), BF16)],
        compiler_params=PARAMS,
        name="early_products",
    )(in_smem(idx), blocks, *ins)


def solve_kernel(front, cols, own_ref, *refs):
    msgs, rhs_ref, inv_ref, out_ref = refs[: cols - 1], refs[cols - 1], refs[cols], refs[cols + 1]
    part, probes, _ = own_ref.shape
    total = [own_ref[k] for k in range(part)]
    for msg in msgs:
        total = [a + b for a, b in zip(total, decode_blocks(msg, part, probes))]
    solved = [
        lax.dot_general(
            rhs_ref[front, k] - total[k],
            inv_ref[front, k],
            (((1,), (0,)), ((), ())),
            precision=lax.Precision.HIGH,
            preferred_element_type=F32,
        )
        for k in range(part)
    ]
    encode_blocks(solved, out_ref, probes)


def solve_part(front, cols, own, msgs, rhs, inverse):
    part, probes, order = own.shape
    return pl.pallas_call(
        functools.partial(solve_kernel, front, cols),
        out_shape=jax.ShapeDtypeStruct((part * probes + SCALES, order), I16),
        in_specs=[VMEM] * (cols + 2),
        out_specs=VMEM,
        compiler_params=PARAMS,
        name=f"solve_{front}",
    )(own, *msgs, rhs, inverse)


def pack_kernel(sources, groups, cap, sel_ref, *refs):
    cols = len(sources)
    msgs, sends, rows = refs[:cols], refs[cols:-1], refs[-1]
    rows_dev, probes, _ = rows.shape
    part = rows_dev // cols
    here = lax.axis_index("cols")
    for mask, msg in zip(sources, msgs):
        first = (here ^ mask) * part
        for k, value in enumerate(decode_blocks(msg, part, probes)):
            rows[first + k] = value.astype(BF16)
    for m in range(groups):
        for q in range(cap):
            sends[m][q * probes : (q + 1) * probes] = rows[sel_ref[q, m * rows_dev]]


def pack(sources, groups, cap, sel, msgs, shape):
    rows_dev, probes, order = shape
    return pl.pallas_call(
        functools.partial(pack_kernel, sources, groups, cap),
        out_shape=[jax.ShapeDtypeStruct((cap * probes, order), BF16)] * groups,
        in_specs=[SMEM] + [VMEM] * len(msgs),
        out_specs=[VMEM] * groups,
        scratch_shapes=[pltpu.VMEM((rows_dev, probes, order), BF16)],
        compiler_params=PARAMS,
        name="pack",
    )(in_smem(sel), *msgs)


def unpack_kernel(front, sources, *refs):
    msgs, out_ref, rows, sems = refs[: len(sources)], refs[-3], refs[-2], refs[-1]
    part, probes, _ = rows.shape[1:]
    here = lax.axis_index("cols")
    copies = []
    for s, (mask, msg) in enumerate(zip(sources, msgs)):
        for k, value in enumerate(decode_blocks(msg, part, probes)):
            rows[s, k] = value
        to = out_ref.at[front, pl.ds((here ^ mask) * part, part)]
        copies.append(pltpu.make_async_copy(rows.at[s], to, sems.at[s]))
        copies[-1].start()
    for copy in copies:
        copy.wait()


def unpack(front, sources, msgs, shape, rows_part, base=None):
    _, _, probes, order = shape
    cols, part = len(sources), rows_part
    rest = [] if base is None else [base]
    return pl.pallas_call(
        functools.partial(unpack_kernel, front, sources),
        out_shape=jax.ShapeDtypeStruct(shape, F32),
        in_specs=[VMEM] * cols + [HBM] * len(rest),
        out_specs=HBM,
        input_output_aliases={} if base is None else {cols: 0},
        scratch_shapes=[
            pltpu.VMEM((cols, part, probes, order), F32),
            pltpu.SemaphoreType.DMA((cols,)),
        ],
        compiler_params=PARAMS,
        name=f"unpack_{front}",
    )(*msgs, *rest)


def shards(groups, cols, owner_map, colidx, live, blocks, diag_inverse, right_side, prior):
    _, rows_dev, slots, order, _ = blocks.shape
    probes = right_side.shape[2]
    prior_dev = prior.shape[0]
    half = groups // 2
    cap = -(-((slots + 1) // 2) * rows_dev // groups)
    def over_rows(x, mask):
        return lax.ppermute(x, "rows", [(i, i ^ mask) for i in range(groups)])

    def over_cols(x, mask):
        return lax.ppermute(x, "cols", [(i, i ^ mask) for i in range(cols)])

    col_order = list(range(cols - 1, 0, -2)) + list(range(cols - 2, 0, -2))
    row_order = list(range(2, groups, 2)) + list(range(3, groups, 2)) + [1]

    def scatter(xs):
        return [over_cols(xs[m - 1], m) for m in col_order]

    def gather(x, masks):
        return [over_cols(x, m) if m else x for m in masks]

    colidx = jnp.transpose(colidx, (2, 0, 1))
    own = start(colidx, prior)
    peers = [m + (m.bit_count() > 1) for m in row_order if m % 2 == 0][::-1]
    chips = [over_rows(own, m) for m in peers]
    blocks0, blocks1, rhs, inverse, alive, first_at = load(
        groups, cols, prior_dev, colidx, live, blocks, right_side, diag_inverse
    )
    chips, blocks0 = lax.optimization_barrier((chips, blocks0))
    held = {0: own} | dict(zip(peers, chips))
    held |= {m ^ 1: over_rows(held[m], 1) for m in [0] + peers[::-1]}
    pieces = [held[2 * k] for k in range(half)] + [held[2 * k + 1] for k in range(half)]
    early_at = [g * prior_dev for g in range(groups)]
    want, second_at = route(groups, cap, slots, prior_dev, owner_map, alive, pieces)

    own0, msgs0 = partial_products(
        "partial_0", cols, probes, first_at, blocks0, pieces, TAIL, early_at
    )
    coded0 = solve_part(0, cols, own0, scatter(msgs0), rhs, inverse)
    sources = [0] + col_order[::-1]
    all0 = gather(coded0, sources)

    place = {m: (m & 1) * half + (m >> 1) for m in range(groups)}
    sends = pack(sources, groups, cap, want, all0, right_side.shape[1:])
    recent = [sends[0]] + [over_rows(sends[place[m]], m) for m in row_order]
    recent_at = [place[m] * cap for m in [0] + row_order]
    early = early_products(probes, second_at, blocks1, pieces, early_at)
    part = rows_dev // cols
    solved = unpack(0, sources, all0, right_side.shape, part)

    own1, msgs1 = partial_products(
        "partial_1",
        cols,
        probes,
        second_at,
        blocks1,
        recent,
        0,
        recent_at,
        groups * prior_dev,
        0,
        [early],
    )
    coded1 = solve_part(1, cols, own1, scatter(msgs1), rhs, inverse)
    sources = [0] + col_order[-2::-1] + col_order[-1:]
    all1 = gather(coded1, sources)
    solved = unpack(1, sources[:-1], all1[:-1], right_side.shape, part, solved)
    return unpack(1, sources[-1:], all1[-1:], right_side.shape, part, solved)


def solution(mesh):
    placed = (
        P(),
        P(None, "rows", "cols"),
        P(None, "rows"),
        P(None, "rows", "cols", None, None),
        P(None, "rows", None, None),
        P(None, "rows", None, None),
        P("rows", None, None),
    )
    body = functools.partial(shards, mesh.shape["rows"], mesh.shape["cols"])
    return jax.shard_map(
        body, mesh=mesh, in_specs=placed, out_specs=P(None, "rows", None, None), check_vma=False
    )
```
